512 devices in a mesh: sub: 128 (over z, y, core), blk: 4 (over x).
Axes of the slice: x: 4, y: 4, z: 16, core: 2. Of those that a mesh axis runs over, the one named last changes fastest.
Arguments:
- rhs: float32 [128, 4, 1024, 256], P('sub', 'blk')
- blocks: float32 [128, 4, 4, 256, 256], P('sub', 'blk')
- coupling: float32 [128, 4, 2, 128, 128], P('sub', 'blk'), may hold values from -0.5 to 0.5
- inverse: float32 [128, 4, 5, 256, 256], P('sub', 'blk')
- deflation: float32 [128, 4, 40, 1024], P('sub', 'blk'), may hold values from -0.1875 to 0.1875
- counts: int32 [128, 4], P('sub', 'blk'), may hold values from 8 to 40
- panel: float32 [128, 160, 160], P('sub')
- intersection_rows: int32 [128, 4, 256], P('sub', 'blk'), may hold values from 0 to 1023, as said below
Outputs:
- solution: float32 [128, 4, 1024, 256], P('sub', 'blk')
- estimate: float32 [256], replicated
The draws below stay inside these ranges and needn't reach their ends.
Inputs may be any that keep to these rules, and one draw needn't show every extreme that they name: `intersection_rows`: the (256) indices of one subdomain are distinct.
All inputs are finite; a program needn't handle non-finite values.
Results may differ from the reference program's by a relative error of at most 0.00015.
Values sent between devices are 32-bit elements; how exact they have to be, the bound alone decides.
No kernel may reach another device: no remote copies, remote signals or barrier semaphores. Data moves between devices by JAX's collectives and lax.ppermute only.
A program may use at most 64 MiB of HBM per device.

```python
import jax
import jax.numpy as jnp
from jax import lax

ROWS = 1024
RHS = 256
BLK = 256
KMAX = 40
KMIN = 8
OVL = 128
N_SUB = 128
N_BLK = 4


def diagonal_heavy(key, shape, lowest, highest_value, spread):
    key_noise, key_diag = jax.random.split(key)
    order = shape[-1]
    noise = jax.random.normal(key_noise, shape, jnp.float32) * (spread / order ** 0.5)
    diag = jax.random.uniform(key_diag, shape[:-1], jnp.float32, lowest, highest_value)
    return noise + jnp.eye(order, dtype=jnp.float32) * diag[..., None]


def draw_blocks(key, part):
    key = jax.random.fold_in(key, 11)
    shape = (N_SUB, N_BLK, ROWS // BLK, BLK, BLK)
    return diagonal_heavy(key, shape, 1.5, 3.0, 0.5)


def draw_inverse(key, part):
    key = jax.random.fold_in(key, 12)
    shape = (N_SUB, N_BLK, ROWS // BLK + 1, BLK, BLK)
    return diagonal_heavy(key, shape, 0.3, 0.8, 0.2)


def draw_panel(key, part):
    key = jax.random.fold_in(key, 13)
    shape = (N_SUB, N_BLK * KMAX, N_BLK * KMAX)
    return diagonal_heavy(key, shape, 1.0, 3.0, 0.6)


def draw_rhs(key, part):
    key = jax.random.fold_in(key, 14)
    key_main = jax.random.fold_in(key, 0)
    ramp = 1.0 + 2.0 * jnp.arange(N_SUB, dtype=jnp.float32) / max(N_SUB - 1, 1)
    ramp = ramp.reshape(N_SUB, 1, 1, 1)
    shape = (N_SUB, N_BLK, ROWS, RHS)
    return jax.random.normal(key_main, shape, jnp.float32) * ramp


def draw_counts(key, part):
    key = jax.random.fold_in(key, 15)
    key_val, key_pos = jax.random.split(key)
    total = N_SUB * N_BLK
    values = jax.random.randint(key_val, (total,), KMIN, KMAX + 1, jnp.int32)
    places = jax.random.permutation(key_pos, total)
    values = values.at[places[0]].set(KMAX)
    values = values.at[places[1]].set(KMIN)
    return values.reshape(N_SUB, N_BLK).astype(jnp.int32)


def draw_intersection_rows(key, part):
    key = jax.random.fold_in(key, 16)
    keys = jax.random.split(key, N_SUB * N_BLK)
    picked = jax.vmap(lambda single: jax.random.permutation(single, ROWS)[:2 * (BLK // 2)])(keys)
    return picked.reshape(N_SUB, N_BLK, 2 * (BLK // 2)).astype(jnp.int32)


def steps_of(stream_key, shape, cuts, least, largest):
    level = 1.0
    for axis_at, blocks in cuts:
        steps = jax.random.uniform(jax.random.fold_in(jax.random.fold_in(stream_key, 6), axis_at), (blocks,), jnp.float32, least / len(cuts), largest / len(cuts))
        level = level * jnp.repeat(jnp.exp(steps), shape[axis_at] // blocks).reshape((-1,) + (1,) * (len(shape) - 1 - axis_at))
    return level


def gaussian(rng, shape, scale, reach, pieces=(), kind=jnp.bfloat16):
    result = scale * jax.random.normal(rng, shape, jnp.float32)
    if pieces:
        result = result * steps_of(rng, shape, pieces, -0.22, 0.18)
    return jnp.clip(result, -reach, reach).astype(kind)


def setup_inputs(seed: int = 0) -> dict:
    arg_keys = jax.random.split(jax.random.key(seed), 9)
    rhs = draw_rhs(jax.random.fold_in(arg_keys[8], 71), 0)
    blocks = draw_blocks(jax.random.fold_in(arg_keys[8], 71), 0)
    coupling = gaussian(arg_keys[2], (N_SUB, N_BLK, 2, OVL, OVL), OVL ** -0.5, 0.5, ((0, 128), (1, 4)), jnp.float32)
    inverse = draw_inverse(jax.random.fold_in(arg_keys[8], 71), 0)
    deflation = gaussian(arg_keys[4], (N_SUB, N_BLK, KMAX, ROWS), ROWS ** -0.5, 0.1875, ((0, 128), (1, 4)), jnp.float32)
    counts = draw_counts(jax.random.fold_in(arg_keys[8], 71), 0)
    panel = draw_panel(jax.random.fold_in(arg_keys[8], 71), 0)
    intersection_rows = draw_intersection_rows(jax.random.fold_in(arg_keys[8], 71), 0)
    return {"rhs": rhs, "blocks": blocks, "coupling": coupling, "inverse": inverse, "deflation": deflation, "counts": counts, "panel": panel, "intersection_rows": intersection_rows}


highest = lax.Precision.HIGHEST

def rows_take(field, index):
    return jax.vmap(jax.vmap(lambda arr, idx: arr[idx]))(field, index)

def rows_add(field, index, values):
    return jax.vmap(jax.vmap(lambda arr, idx, val: arr.at[idx].add(val)))(field, index, values)

def from_sides(sent_low, sent_high):
    zero = jnp.zeros_like(sent_low[:1])
    from_low = jnp.concatenate([zero, sent_high[:-1]], 0)
    from_high = jnp.concatenate([sent_low[1:], zero], 0)
    return (from_low, from_high)

def apply_operator(field, blocks, coupling, intersection_rows):
    nsub, nblk, nrows, ncols = field.shape
    width = blocks.shape[3]
    half = intersection_rows.shape[2] // 2
    low_idx = intersection_rows[:, :, :half]
    high_idx = intersection_rows[:, :, half:]
    from_low, from_high = from_sides(rows_take(field, low_idx), rows_take(field, high_idx))
    local = jnp.einsum('sbnij,sbnjr->sbnir', blocks, field.reshape(nsub, nblk, -1, width, ncols), precision=highest)
    local = local.reshape(nsub, nblk, nrows, ncols)
    near_low = jnp.einsum('sbij,sbjr->sbir', coupling[:, :, 0], from_low, precision=highest)
    near_high = jnp.einsum('sbij,sbjr->sbir', coupling[:, :, 1], from_high, precision=highest)
    local = rows_add(local, low_idx, near_low)
    return rows_add(local, high_idx, near_high)

def apply_precond(resid, inverse, masked, panel, intersection_rows):
    nsub, nblk, nrows, ncols = resid.shape
    width = inverse.shape[3]
    half = intersection_rows.shape[2] // 2
    low_idx = intersection_rows[:, :, :half]
    high_idx = intersection_rows[:, :, half:]
    from_low, from_high = from_sides(rows_take(resid, low_idx), rows_take(resid, high_idx))
    extended = jnp.concatenate([from_low, resid, from_high], 2)
    solved = jnp.einsum('sbnij,sbnjr->sbnir', inverse, extended.reshape(nsub, nblk, -1, width, ncols), precision=highest)
    solved = solved.reshape(nsub, nblk, nrows + 2 * half, ncols)
    own = solved[:, :, half:half + nrows]
    back_low = solved[:, :, :half]
    back_high = solved[:, :, half + nrows:]
    zero = jnp.zeros_like(back_low[:1])
    into_high = jnp.concatenate([back_low[1:], zero], 0)
    into_low = jnp.concatenate([zero, back_high[:-1]], 0)
    own = rows_add(own, low_idx, into_low)
    own = rows_add(own, high_idx, into_high)
    coef = jnp.einsum('sbkn,sbnr->sbkr', masked, resid, precision=highest)
    kmax = coef.shape[2]
    stacked = coef.reshape(nsub, nblk * kmax, ncols)
    correct = jnp.einsum('sij,sjr->sir', panel, stacked, precision=highest).reshape(nsub, nblk, kmax, ncols)
    return own + jnp.einsum('sbkn,sbkr->sbnr', masked, correct, precision=highest)

def least_squares(beta, proj_one, sub_one, proj_two_a, proj_two_b, sub_two):
    diag_one = jnp.sqrt(proj_one * proj_one + sub_one * sub_one)
    cross = (proj_one * proj_two_a + sub_one * proj_two_b) / diag_one
    rest_a = proj_two_a - cross * proj_one / diag_one
    rest_b = proj_two_b - cross * sub_one / diag_one
    diag_two = jnp.sqrt(rest_a * rest_a + rest_b * rest_b + sub_two * sub_two)
    coeff_two = beta * rest_a / (diag_two * diag_two)
    coeff_one = (beta * proj_one / diag_one - cross * coeff_two) / diag_one
    miss_a = beta - proj_one * coeff_one - proj_two_a * coeff_two
    miss_b = sub_one * coeff_one + proj_two_b * coeff_two
    miss_c = sub_two * coeff_two
    miss = jnp.sqrt(miss_a * miss_a + miss_b * miss_b + miss_c * miss_c)
    return (coeff_one, coeff_two, miss)

def reference(rhs, blocks, coupling, inverse, deflation, counts, panel, intersection_rows):
    kmax = deflation.shape[2]
    keep = (jnp.arange(kmax, dtype=jnp.int32)[None, None, :] < counts[:, :, None]).astype(jnp.float32)
    masked = deflation * keep[..., None]
    axes_all = (0, 1, 2)
    beta = jnp.sqrt(lax.optimization_barrier(jnp.sum(rhs * rhs, axes_all)))
    basis_one = rhs / beta
    search_one = apply_precond(basis_one, inverse, masked, panel, intersection_rows)
    image = apply_operator(search_one, blocks, coupling, intersection_rows)
    proj_one = lax.optimization_barrier(jnp.sum(image * basis_one, axes_all))
    image_sq = lax.optimization_barrier(jnp.sum(image * image, axes_all))
    sub_one = jnp.sqrt(image_sq - proj_one * proj_one)
    basis_two = (image - proj_one * basis_one) / sub_one
    search_two = apply_precond(basis_two, inverse, masked, panel, intersection_rows)
    image_two = apply_operator(search_two, blocks, coupling, intersection_rows)
    proj_two_a = lax.optimization_barrier(jnp.sum(image_two * basis_one, axes_all))
    proj_two_b = lax.optimization_barrier(jnp.sum(image_two * basis_two, axes_all))
    image_two_sq = lax.optimization_barrier(jnp.sum(image_two * image_two, axes_all))
    sub_two = jnp.sqrt(image_two_sq - proj_two_a * proj_two_a - proj_two_b * proj_two_b)
    coeff_one, coeff_two, miss = least_squares(beta, proj_one, sub_one, proj_two_a, proj_two_b, sub_two)
    solution = coeff_one * search_one + coeff_two * search_two
    return (solution, miss)
```

```python
import functools

import jax
import jax.numpy as jnp
from jax import lax
from jax.experimental import pallas as pl
from jax.experimental.pallas import tpu as pltpu
from jax.sharding import PartitionSpec as P

f32 = jnp.float32
bf16 = jnp.bfloat16
AXES = ("sub", "blk")
LIMIT = 24 * 1024 * 1024


def split(a):
    high = a.astype(bf16)
    return high, (a - high.astype(f32)).astype(bf16)


def dot(a, b, dims=((1,), (0,))):
    return lax.dot_general(a, b, (dims, ((), ())), preferred_element_type=f32)


def mul(a, b, dims=((1,), (0,))):
    return dot(a[0], b[0], dims) + (dot(a[0], b[1], dims) + dot(a[1], b[0], dims))


def pick(onehot, b):
    return dot(onehot, b[0]) + dot(onehot, b[1])


def gather_matrix(idx, nrows):
    count = idx.shape[1]
    column = jnp.broadcast_to(idx.astype(f32), (128, count)).T
    lane = lax.broadcasted_iota(jnp.int32, (count, 128), 1).astype(f32)
    parts = [
        jnp.where(column == lane + float(128 * k), 1.0, 0.0).astype(bf16)
        for k in range(nrows // 128)
    ]
    return jnp.concatenate(parts, axis=1)


def scatter_matrix(idx, nrows):
    row = lax.broadcasted_iota(jnp.int32, (nrows, idx.shape[1]), 0)
    return jnp.where(row == idx, 1.0, 0.0).astype(bf16)


def masked_deflation(defl_ref, count):
    kmax, nrows = defl_ref.shape
    row = lax.broadcasted_iota(jnp.int32, (kmax, nrows), 0)
    return jnp.where(row < count, defl_ref[...], 0.0)


def prep_kernel(scal_ref, r_ref, idx_ref, defl_ref, inv_ref, up_ref, dn_ref, coef_ref):
    half = idx_ref.shape[1] // 2
    nrows = r_ref.shape[0]
    r = split(r_ref[...])
    rows = pick(gather_matrix(idx_ref[...], nrows), r)
    dn_ref[:half] = rows[:half]
    up_ref[:half] = rows[half:]
    dn_ref[half : 2 * half] = r_ref[:half]
    up_ref[half : 2 * half] = r_ref[nrows - half :]
    dn_ref[2 * half :] = inv_ref[0, :half]
    up_ref[2 * half :] = inv_ref[inv_ref.shape[0] - 1, inv_ref.shape[1] - half :]
    coef = mul(split(masked_deflation(defl_ref, scal_ref[0])), r)
    for k in range(coef_ref.shape[0]):
        coef_ref[k] = coef


def local_kernel(
    scal_ref, r_ref, up_ref, dn_ref, lo_ref, hi_ref, inv_lo_ref, inv_hi_ref, inv_ref, all_ref,
    panel_ref, defl_ref, idx_ref, z_ref, zup_ref, zdn_ref,
):
    half = idx_ref.shape[1] // 2
    nrows, ncols = r_ref.shape
    kmax = defl_ref.shape[0]
    width = inv_ref.shape[1]
    idx = idx_ref[...]
    r_first, r_last = r_ref[:half], r_ref[nrows - half :]
    back_lo = mul(split(inv_lo_ref[2 * half :]), split(jnp.concatenate([lo_ref[half : 2 * half], dn_ref[:half]], 0)))
    back_hi = mul(split(inv_hi_ref[2 * half :]), split(jnp.concatenate([up_ref[:half], hi_ref[half : 2 * half]], 0)))
    back = split(jnp.concatenate([back_lo, back_hi], 0))
    slot = pl.multiple_of(scal_ref[1] * kmax, 8)
    panel = split(panel_ref[pl.ds(slot, kmax), :])
    coefs = split(all_ref[...].reshape(all_ref.shape[0] * kmax, ncols))
    coarse = split(mul(panel, coefs))
    masked = split(masked_deflation(defl_ref, scal_ref[0]))
    z_ref[...] = mul(masked, coarse, ((0,), (0,))) + pick(scatter_matrix(idx, nrows), back)
    last = inv_ref.shape[0] - 1
    for n in range(last + 1):
        if n == 0:
            part = jnp.concatenate([lo_ref[:half], r_first], 0)
        elif n == last:
            part = jnp.concatenate([r_last, hi_ref[:half]], 0)
        else:
            part = r_ref[n * width - half : (n + 1) * width - half]
        low = half if n == 0 else 0
        high = width - half if n == last else width
        y = mul(split(inv_ref[n][low:high]), split(part))
        at = n * width + low - half
        z_ref[at : at + high - low] += y
    rows = pick(gather_matrix(idx, nrows), split(z_ref[...]))
    zdn_ref[...] = rows[:half]
    zup_ref[...] = rows[half:]


def blocks_kernel(scal_ref, z_ref, mats_ref, defl_ref, idx_ref, t_ref, rows_ref, coef_ref):
    width = mats_ref.shape[1]
    nrows = z_ref.shape[0]
    for n in range(mats_ref.shape[0]):
        part = slice(n * width, (n + 1) * width)
        t_ref[part] = mul(split(mats_ref[n]), split(z_ref[part]))
    t = split(t_ref[...])
    rows_ref[...] = pick(gather_matrix(idx_ref[...], nrows), t)
    coef_ref[...] = mul(split(masked_deflation(defl_ref, scal_ref[0])), t)


def near_rows(couple_ref, lo_ref, hi_ref):
    near_lo = mul(split(couple_ref[0]), split(lo_ref[...]))
    near_hi = mul(split(couple_ref[1]), split(hi_ref[...]))
    return jnp.concatenate([near_lo, near_hi], 0)


def image_kernel(
    scal_ref, t_ref, rows_ref, tcoef_ref, couple_ref, lo_ref, hi_ref, defl_ref, idx_ref,
    u_ref, up_ref, dn_ref, coef_ref,
):
    half = idx_ref.shape[1] // 2
    nrows = t_ref.shape[0]
    near = near_rows(couple_ref, lo_ref, hi_ref)
    rows = rows_ref[...] + near
    near = split(near)
    scatter = scatter_matrix(idx_ref[...], nrows)
    spread = pick(scatter, near)
    u_ref[...] = t_ref[...] + spread
    dn_ref[:half] = rows[:half]
    up_ref[:half] = rows[half:]
    dn_ref[half:] = u_ref[:half]
    up_ref[half:] = u_ref[nrows - half :]
    coef = tcoef_ref[...] + mul(split(masked_deflation(defl_ref, scal_ref[0])), split(spread))
    for k in range(coef_ref.shape[0]):
        coef_ref[k] = coef


def inverse_or_zero(a):
    return jnp.where(a > 0.0, 1.0 / jnp.where(a > 0.0, a, 1.0), 0.0)


def total(a):
    return jnp.sum(a, axis=0, keepdims=True)


def gram_kernel(t_ref, couple_ref, lo_ref, hi_ref, idx_ref, u0_ref, u1_ref, out_ref):
    nrows = t_ref.shape[0]
    near = split(near_rows(couple_ref, lo_ref, hi_ref))
    u2 = t_ref[...] + pick(scatter_matrix(idx_ref[...], nrows), near)
    u0, u1 = u0_ref[...], u1_ref[...]
    unit, length = [], []
    for u in (u0, u1, u2):
        top = jnp.max(jnp.abs(u), axis=0, keepdims=True)
        scaled = u * inverse_or_zero(top)
        size = jnp.sqrt(total(scaled * scaled))
        unit.append((scaled, inverse_or_zero(size)))
        length.append(top * size)
    rows = list(length)
    for i, j in ((0, 1), (0, 2), (1, 2)):
        rows.append(total(unit[i][0] * unit[j][0]) * unit[i][1] * unit[j][1])
    rows += [jnp.zeros_like(rows[0])] * 2
    full = jnp.concatenate(rows, 0)
    for k in range(out_ref.shape[0]):
        out_ref[k] = full


def merge(parts):
    lengths, shares = [], []
    for i in range(3):
        own = parts[:, i, :]
        top = jnp.max(own, axis=0, keepdims=True)
        share = own * inverse_or_zero(top)
        size = jnp.sqrt(total(share * share))
        lengths.append(top * size)
        shares.append(share * inverse_or_zero(size))
    cosines = [
        total(parts[:, 3 + k, :] * shares[i] * shares[j])
        for k, (i, j) in enumerate(((0, 1), (0, 2), (1, 2)))
    ]
    return lengths, cosines


def merge_kernel(parts_ref, out_ref):
    lengths, cosines = merge(parts_ref[...])
    rows = lengths + cosines
    full = jnp.concatenate(rows + [jnp.zeros_like(rows[0])] * 2, 0)
    for k in range(out_ref.shape[0]):
        out_ref[k] = full


def least_squares(beta, proj_one, sub_one, proj_two_a, proj_two_b, sub_two):
    diag_one = jnp.sqrt(proj_one * proj_one + sub_one * sub_one)
    cross = (proj_one * proj_two_a + sub_one * proj_two_b) / diag_one
    rest_a = proj_two_a - cross * proj_one / diag_one
    rest_b = proj_two_b - cross * sub_one / diag_one
    diag_two = jnp.sqrt(rest_a * rest_a + rest_b * rest_b + sub_two * sub_two)
    coeff_two = beta * rest_a / (diag_two * diag_two)
    coeff_one = (beta * proj_one / diag_one - cross * coeff_two) / diag_one
    miss_a = beta - proj_one * coeff_one - proj_two_a * coeff_two
    miss_b = sub_one * coeff_one + proj_two_b * coeff_two
    miss_c = sub_two * coeff_two
    miss = jnp.sqrt(miss_a * miss_a + miss_b * miss_b + miss_c * miss_c)
    return (coeff_one, coeff_two, miss)


def finish_kernel(parts_ref, p_ref, q_ref, out_ref, miss_ref):
    (beta, len_one, len_two), (cos_01, cos_02, cos_12) = merge(parts_ref[...])
    rel_one = len_one / beta
    proj_one = rel_one * cos_01
    sine_sq = 1.0 - cos_01 * cos_01
    sub_one = rel_one * jnp.sqrt(sine_sq)
    rel_two = len_two / beta / sub_one
    proj_two_a = rel_two * cos_02 - proj_one * (proj_one / sub_one)
    side = (cos_12 - cos_01 * cos_02) / jnp.sqrt(sine_sq)
    proj_two_b = rel_two * side - proj_one
    sub_two = rel_two * jnp.sqrt(1.0 - cos_02 * cos_02 - side * side)
    coeff_one, coeff_two, miss = least_squares(beta, proj_one, sub_one, proj_two_a, proj_two_b, sub_two)
    miss_ref[...] = miss
    second = coeff_two / sub_one
    first = (coeff_one - second * proj_one) / beta
    out_ref[...] = first * p_ref[...] + (second / beta) * q_ref[...]


def shape(*dims):
    return jax.ShapeDtypeStruct(dims, f32)


def call(kernel, out_shape, *operands, specs=None, flops=0):
    extra = {} if specs is None else {"in_specs": specs}
    size = sum(4 * a.size for a in operands)
    return pl.pallas_call(
        kernel,
        out_shape=out_shape,
        compiler_params=pltpu.CompilerParams(vmem_limit_bytes=LIMIT),
        cost_estimate=pl.CostEstimate(flops=flops, bytes_accessed=size, transcendentals=0),
        name=kernel.__name__,
        **extra,
    )(*operands)


VMEM = pl.BlockSpec(memory_space=pltpu.VMEM)
SMEM = pl.BlockSpec(memory_space=pltpu.SMEM)


def body(mesh, rhs, blocks, coupling, inverse, deflation, counts, panel, intersection_rows):
    source, mats, couple, inv = rhs[0, 0], blocks[0, 0], coupling[0, 0], inverse[0, 0]
    defl, panel_mat = deflation[0, 0], panel[0]
    idx = intersection_rows[0]
    half = idx.shape[1] // 2
    nrows, ncols = source.shape
    kmax = defl.shape[0]
    n_sub, n_blk = mesh.shape["sub"], mesh.shape["blk"]
    scal = jnp.stack([counts[0, 0], lax.axis_index("blk").astype(jnp.int32)])
    up = [(i, i + 1) for i in range(n_sub - 1)]
    down = [(i + 1, i) for i in range(n_sub - 1)]

    def halo(to_up, to_down):
        return lax.ppermute(to_up, "sub", up), lax.ppermute(to_down, "sub", down)

    def coarse_group(coef):
        return lax.all_to_all(coef, "blk", 0, 0)

    def precond(vector, sent, got, coefs, inv_lo, inv_hi):
        return call(
            local_kernel, (shape(nrows, ncols), shape(half, ncols), shape(half, ncols)),
            scal, vector, sent[0], sent[1], got[0], got[1], inv_lo, inv_hi, inv, coefs, panel_mat,
            defl, idx, specs=[SMEM] + [VMEM] * 12, flops=10**9,
        )

    def diagonal(field):
        return call(
            blocks_kernel, (shape(nrows, ncols), shape(2 * half, ncols), shape(kmax, ncols)),
            scal, field, mats, defl, idx, specs=[SMEM] + [VMEM] * 4, flops=10**9,
        )

    sent_up, sent_dn, coef = call(
        prep_kernel,
        (shape(3 * half, ncols), shape(3 * half, ncols), shape(n_blk, kmax, ncols)),
        scal, source, idx, defl, inv, specs=[SMEM] + [VMEM] * 4,
        flops=3 * 10**8,
    )
    got_lo, got_hi = halo(sent_up, sent_dn)
    coefs = coarse_group(coef)
    inv_lo, inv_hi = got_lo, got_hi
    search_one, z_up, z_dn = precond(source, (sent_up, sent_dn), (got_lo, got_hi), coefs, inv_lo, inv_hi)
    z_lo, z_hi = halo(z_up, z_dn)
    diag, diag_rows, diag_coef = diagonal(search_one)
    image, sent_up, sent_dn, coef = call(
        image_kernel,
        (shape(nrows, ncols), shape(2 * half, ncols), shape(2 * half, ncols), shape(n_blk, kmax, ncols)),
        scal, diag, diag_rows, diag_coef, couple, z_lo, z_hi, defl, idx,
        specs=[SMEM] + [VMEM] * 8, flops=5 * 10**8,
    )
    got_lo, got_hi = halo(sent_up, sent_dn)
    coefs = coarse_group(coef)
    search_two, z_up, z_dn = precond(image, (sent_up, sent_dn), (got_lo, got_hi), coefs, inv_lo, inv_hi)
    z_lo, z_hi = halo(z_up, z_dn)
    diag, _, _ = diagonal(search_two)
    plane, depth = sum_groups(mesh)
    partial_sums = call(
        gram_kernel, shape(len(plane[0]), 8, ncols),
        diag, couple, z_lo, z_hi, idx, source, image, flops=5 * 10**8,
    )
    partial_sums = lax.all_to_all(partial_sums, AXES, 0, 0, axis_index_groups=plane)
    partial_sums = call(merge_kernel, shape(len(depth[0]), 8, ncols), partial_sums)
    partial_sums = lax.all_to_all(partial_sums, AXES, 0, 0, axis_index_groups=depth)
    answer, miss = call(
        finish_kernel, (shape(nrows, ncols), shape(1, ncols)), partial_sums, search_one, search_two
    )
    return (answer[None, None], miss[0])


def sum_groups(mesh):
    n_sub, n_blk = mesh.shape["sub"], mesh.shape["blk"]
    near = min(8, n_sub)
    size = near * n_blk
    count = n_sub // near
    plane = [[g * size + k for k in range(size)] for g in range(count)]
    depth = [[g * size + k for g in range(count)] for k in range(size)]
    return plane, depth


def solution(mesh):
    placed = (
        P("sub", "blk", None, None),
        P("sub", "blk", None, None, None),
        P("sub", "blk", None, None, None),
        P("sub", "blk", None, None, None),
        P("sub", "blk", None, None),
        P("sub", "blk"),
        P("sub", None, None),
        P("sub", "blk", None),
    )
    return jax.shard_map(
        functools.partial(body, mesh),
        mesh=mesh,
        in_specs=placed,
        out_specs=(P("sub", "blk", None, None), P()),
        check_vma=False,
    )
```

```python
import functools

import jax
import jax.numpy as jnp
from jax import lax
from jax.experimental import pallas as pl
from jax.experimental.pallas import tpu as pltpu
from jax.sharding import PartitionSpec as P

f32 = jnp.float32
bf16 = jnp.bfloat16
AXES = ("sub", "blk")
WIDE = 128
LIMIT = 24 * 1024 * 1024


def split(a):
    high = a.astype(bf16)
    return high, (a - high.astype(f32)).astype(bf16)


def dot(a, b, dims=((1,), (0,))):
    return lax.dot_general(a, b, (dims, ((), ())), preferred_element_type=f32)


def mul(a, b, dims=((1,), (0,))):
    return dot(a[0], b[0], dims) + (dot(a[0], b[1], dims) + dot(a[1], b[0], dims))


def pick(onehot, b):
    return dot(onehot, b[0]) + dot(onehot, b[1])


def gather_matrix(idx, nrows):
    count = idx.shape[1]
    column = jnp.broadcast_to(idx.astype(f32), (128, count)).T
    lane = lax.broadcasted_iota(jnp.int32, (count, 128), 1).astype(f32)
    parts = [
        jnp.where(column == lane + float(128 * k), 1.0, 0.0).astype(bf16)
        for k in range(nrows // 128)
    ]
    return jnp.concatenate(parts, axis=1)


def scatter_matrix(idx, nrows):
    row = lax.broadcasted_iota(jnp.int32, (nrows, idx.shape[1]), 0)
    return jnp.where(row == idx, 1.0, 0.0).astype(bf16)


def masked_deflation(defl, count):
    row = lax.broadcasted_iota(jnp.int32, defl.shape, 0)
    return jnp.where(row < count, defl, 0.0)


def edge_block(high, ref, width):
    start = pl.multiple_of(jnp.where(high, ref.shape[0] - width, 0), width)
    return ref[pl.ds(start, width)]


def padded(a, count):
    return jnp.concatenate([a, jnp.zeros((count - a.shape[0], a.shape[1]), a.dtype)], 0)


def tripled(high, low):
    return padded(jnp.concatenate([high, high, low], 0), WIDE).astype(bf16)


def gather_all(gather_ref, many, lines, a):
    high, low = split(a)
    top = dot(gather_ref[...], high)
    rest = dot(gather_ref[: many + lines], low)
    return top[:many] + rest[:many], top[many : many + lines] + (top[many + lines :] + rest[many:])


def prep_kernel(
    count_ref, odd_ref, slot_ref, r_hbm, idx_hbm, defl_hbm, inv_hbm,
    far_ref, near_ref, coef_ref, r_ref, inv_ref, gather_ref, scatter_ref, zrows_ref, lift_ref, off_ref,
    idx_ref, defl_ref, sems,
):
    many = idx_ref.shape[1]
    half = many // 2
    nrows, ncols = r_ref.shape
    kmax = defl_ref.shape[0]
    lines = zrows_ref.shape[0] // 2
    step = nrows // 4
    blocks, width = inv_ref.shape[0], inv_ref.shape[2]
    odd = odd_ref[0] == 1
    pieces = [(idx_hbm, idx_ref), (defl_hbm, defl_ref)]
    pieces += [(r_hbm.at[pl.ds(k * step, step)], r_ref.at[pl.ds(k * step, step)]) for k in range(4)]
    pieces += [(inv_hbm.at[k], inv_ref.at[k]) for k in (0, blocks - 1)]
    pieces += [(inv_hbm.at[pl.ds(1, blocks - 2)], inv_ref.at[pl.ds(1, blocks - 2)])]
    copies = [pltpu.make_async_copy(a, b, sems.at[k]) for k, (a, b) in enumerate(pieces)]
    for copy in copies[:8]:
        copy.start()
    copies[0].wait()
    low, high = idx_ref[:, :half], idx_ref[:, half:]
    idx = jnp.concatenate([jnp.where(odd, low, high), jnp.where(odd, high, low)], 1)
    gather = gather_matrix(idx, nrows)
    scatter = scatter_matrix(idx, nrows)
    gather_ref[:many] = gather
    scatter_ref[:, :many] = scatter
    off_ref[...] = 1.0 - dot(scatter, jnp.ones((many, off_ref.shape[1]), bf16))
    copies[1].wait()
    masked = masked_deflation(defl_ref[...], count_ref[0, 0])
    z_high = masked.astype(bf16).astype(f32)
    z_low = (masked - z_high).astype(bf16).astype(f32)
    z_pair = jnp.concatenate([padded(z_high, lines), padded(z_low, lines)], 0).astype(bf16)
    gather_ref[many:] = z_pair
    zrows_ref[...] = dot(z_pair, scatter).astype(bf16)
    lift = padded(jnp.concatenate([z_high, z_low, z_high], 0), WIDE).T.astype(bf16)
    scatter_ref[:, many:] = lift
    lift_ref[...] = dot(gather, lift).astype(bf16)
    for copy in copies[2:6]:
        copy.wait()
    copies[8].start()
    rows, coef = gather_all(gather_ref, many, lines, r_ref[...])
    for k in range(coef_ref.shape[0]):
        coef_ref[k] = coef[:kmax]
    copies[6].wait()
    copies[7].wait()
    for k, (ref, high) in enumerate(((near_ref, odd_ref[0] == 0), (far_ref, odd))):
        ref[:half] = rows[k * half : (k + 1) * half]
        ref[half : 2 * half] = edge_block(high, r_ref, half)
        first, last = inv_ref[0, :half], inv_ref[blocks - 1, width - half :]
        ref[2 * half :, :half] = jnp.where(high, last[:, half:], first[:, :half])
        ref[2 * half :, half:] = jnp.where(high, last[:, :half], first[:, half:])
    copies[8].wait()


def local_kernel(
    odd_ref, slot_ref, r_ref, far_ref, near_ref, gfar_ref, gnear_ref, inv_far_ref, inv_near_ref,
    inv_ref, all_ref, panel_ref, lift_ref, gather_ref, own_ref, back_ref, coarse_ref, zfar_ref, znear_ref,
):
    odd = odd_ref[0] == 1
    half = znear_ref.shape[0]
    nrows, ncols = r_ref.shape
    kmax = all_ref.shape[1]
    width = inv_ref.shape[1]
    last = inv_ref.shape[0] - 1
    slot = pl.multiple_of(slot_ref[0] * kmax, 8)
    panel = split(panel_ref[pl.ds(slot, kmax), :])
    coefs = split(all_ref[...].reshape(all_ref.shape[0] * kmax, ncols))
    coarse = mul(panel, coefs)
    high = coarse.astype(bf16).astype(f32)
    coarse = tripled(high, coarse - high)
    coarse_ref[...] = coarse
    rows = dot(lift_ref[...], coarse)
    got_lo = jnp.where(odd, gnear_ref[:half], gfar_ref[:half])
    got_hi = jnp.where(odd, gfar_ref[:half], gnear_ref[:half])
    for n in range(last + 1):
        low = half if n == 0 else 0
        high = width - half if n == last else width
        if n == 0:
            part = jnp.concatenate([got_lo, r_ref[:half]], 0)
        elif n == last:
            part = jnp.concatenate([r_ref[nrows - half :], got_hi], 0)
        else:
            part = r_ref[n * width - half : (n + 1) * width - half]
        at = slice(n * width + low - half, n * width + high - half)
        y = mul(split(inv_ref[n, low:high]), split(part))
        own_ref[at] = y
        rows = rows + pick(gather_ref[: 2 * half, at], split(y))
    back = [
        mul(split(inverse[2 * half :]), split(jnp.concatenate([own[:half], got[half : 2 * half]], 0)))
        for own, got, inverse in ((near_ref, gnear_ref, inv_near_ref), (far_ref, gfar_ref, inv_far_ref))
    ]
    back = jnp.concatenate(back, 0)
    back_ref[...] = back
    rows = rows + back
    znear_ref[...] = rows[:half]
    zfar_ref[...] = rows[half:]


def block_products(own_ref, back_ref, coarse_ref, mats_ref, scatter_ref, z_ref, t_ref):
    many = back_ref.shape[0]
    high, low = split(back_ref[...])
    width = mats_ref.shape[1]
    both = jnp.concatenate([high, coarse_ref[...]], 0)
    for n in range(mats_ref.shape[0]):
        part = slice(n * width, (n + 1) * width)
        z = own_ref[part] + (dot(scatter_ref[part], both) + dot(scatter_ref[part, :many], low))
        z_ref[part] = z
        t_ref[part] = mul(split(mats_ref[n]), split(z))


def blocks_kernel(
    own_ref, back_ref, coarse_ref, mats_ref, scatter_ref, gather_ref, z_ref, t_ref, rows_ref, coef_ref
):
    block_products(own_ref, back_ref, coarse_ref, mats_ref, scatter_ref, z_ref, t_ref)
    rows_ref[...], coef = gather_all(gather_ref, rows_ref.shape[0], coef_ref.shape[0], t_ref[...])
    coef_ref[...] = coef


def shared_rows(odd_ref, couple_ref, gfar_ref, gnear_ref):
    near = mul(split(couple_ref[1 - odd_ref[0]]), split(gnear_ref[...]))
    far = mul(split(couple_ref[odd_ref[0]]), split(gfar_ref[...]))
    return jnp.concatenate([near, far], 0)


def image_kernel(
    odd_ref, t_ref, rows_ref, tcoef_ref, zrows_ref, couple_ref, gfar_ref, gnear_ref, scatter_ref,
    u_ref, far_ref, near_ref, coef_ref, urows_ref,
):
    add = shared_rows(odd_ref, couple_ref, gfar_ref, gnear_ref)
    many = add.shape[0]
    half = many // 2
    lines = tcoef_ref.shape[0]
    rows = rows_ref[...] + add
    urows_ref[...] = rows
    high, low = split(add)
    u_ref[...] = t_ref[...] + (dot(scatter_ref[:, :many], high) + dot(scatter_ref[:, :many], low))
    near_ref[:half] = rows[:half]
    far_ref[:half] = rows[half:]
    near_ref[half:] = edge_block(odd_ref[0] == 0, u_ref, half)
    far_ref[half:] = edge_block(odd_ref[0] == 1, u_ref, half)
    coef = dot(zrows_ref[...], high)
    coef = tcoef_ref[...] + (coef[:lines] + (coef[lines:] + dot(zrows_ref[:lines], low)))
    for k in range(coef_ref.shape[0]):
        coef_ref[k] = coef[: coef_ref.shape[1]]


def inverse_or_zero(a):
    return jnp.where(a > 0.0, 1.0 / jnp.where(a > 0.0, a, 1.0), 0.0)


def total(a):
    return jnp.sum(a, axis=0, keepdims=True)


PAIRS = ((0, 1), (0, 2), (1, 2))


def stacked(rows):
    return jnp.concatenate(rows + [jnp.zeros_like(rows[0])] * (8 - len(rows)), 0)


def last_blocks_kernel(
    own_ref, back_ref, coarse_ref, mats_ref, scatter_ref, gather_ref, off_ref,
    u0_ref, u1_ref, far0_ref, near0_ref, rows1_ref,
    z_ref, rows_ref, unit0_ref, unit1_ref, sums_ref, t_ref,
):
    many, ncols = rows_ref.shape
    half = many // 2
    nrows = z_ref.shape[0]
    lanes = off_ref.shape[1]
    block_products(own_ref, back_ref, coarse_ref, mats_ref, scatter_ref, z_ref, t_ref)
    rows_ref[...] = pick(gather_ref[:many], split(t_ref[...]))
    for at in range(0, nrows, 8):
        keep = off_ref[at : at + 8]
        for col in range(0, ncols, lanes):
            t_ref[at : at + 8, col : col + lanes] *= keep
    tops, factors = [], []
    for ref in (u0_ref, u1_ref, t_ref):
        top = jnp.max(jnp.abs(ref[...]).reshape(nrows // 8, 8, ncols), axis=0)
        top = jnp.max(top, axis=0, keepdims=True)
        tops.append(top)
        factors.append(inverse_or_zero(top))
    pairs = ((0, 0), (1, 1), (0, 1), (2, 2), (0, 2), (1, 2))
    sums = [jnp.zeros((8, ncols), f32)] * len(pairs)
    for at in range(0, nrows, 8):
        now = [ref[at : at + 8] * factor for ref, factor in zip((u0_ref, u1_ref, t_ref), factors)]
        sums = [total_ + now[i] * now[j] for total_, (i, j) in zip(sums, pairs)]
    sum_00, sum_11, sum_01, sum_22, sum_02, sum_12 = (total(a) for a in sums)
    size0, size1 = jnp.sqrt(sum_00), jnp.sqrt(sum_11)
    shrink0, shrink1 = inverse_or_zero(size0), inverse_or_zero(size1)
    unit0_ref[:half] = near0_ref[:half] * factors[0] * shrink0
    unit0_ref[half:] = far0_ref[:half] * factors[0] * shrink0
    unit1_ref[...] = rows1_ref[...] * factors[1] * shrink1
    sums_ref[...] = stacked(
        [
            tops[0] * size0, tops[1] * size1, tops[2], sum_01 * shrink0 * shrink1,
            sum_22, sum_02 * shrink0, sum_12 * shrink1,
        ]
    )


def gram_kernel(odd_ref, rows_ref, couple_ref, gfar_ref, gnear_ref, unit0_ref, unit1_ref, sums_ref, out_ref):
    rows = rows_ref[...] + shared_rows(odd_ref, couple_ref, gfar_ref, gnear_ref)
    len0, len1, top_off, cos_01, sum_22, sum_02, sum_12 = (sums_ref[k : k + 1] for k in range(7))
    top = jnp.maximum(top_off, jnp.max(jnp.abs(rows), axis=0, keepdims=True))
    scale = inverse_or_zero(top)
    rows = rows * scale
    ratio = top_off * scale
    size = jnp.sqrt(sum_22 * (ratio * ratio) + total(rows * rows))
    shrink = inverse_or_zero(size)
    cos_02 = (sum_02 * ratio + total(unit0_ref[...] * rows)) * shrink
    cos_12 = (sum_12 * ratio + total(unit1_ref[...] * rows)) * shrink
    full = stacked([len0, len1, top * size, cos_01, cos_02, cos_12])
    for k in range(out_ref.shape[0]):
        out_ref[k] = full


def merge(parts):
    lengths, shares = [], []
    for i in range(3):
        own = parts[:, i, :]
        top = jnp.max(own, axis=0, keepdims=True)
        share = own * inverse_or_zero(top)
        size = jnp.sqrt(total(share * share))
        lengths.append(top * size)
        shares.append(share * inverse_or_zero(size))
    cosines = [
        total(parts[:, 3 + k, :] * shares[i] * shares[j])
        for k, (i, j) in enumerate(PAIRS)
    ]
    return lengths, cosines


def merge_kernel(parts_ref, out_ref):
    lengths, cosines = merge(parts_ref[...])
    full = stacked(lengths + cosines)
    for k in range(out_ref.shape[0]):
        out_ref[k] = full


def least_squares(beta, proj_one, sub_one, proj_two_a, proj_two_b, sub_two):
    diag_one = jnp.sqrt(proj_one * proj_one + sub_one * sub_one)
    cross = (proj_one * proj_two_a + sub_one * proj_two_b) / diag_one
    rest_a = proj_two_a - cross * proj_one / diag_one
    rest_b = proj_two_b - cross * sub_one / diag_one
    diag_two = jnp.sqrt(rest_a * rest_a + rest_b * rest_b + sub_two * sub_two)
    coeff_two = beta * rest_a / (diag_two * diag_two)
    coeff_one = (beta * proj_one / diag_one - cross * coeff_two) / diag_one
    miss_a = beta - proj_one * coeff_one - proj_two_a * coeff_two
    miss_b = sub_one * coeff_one + proj_two_b * coeff_two
    miss_c = sub_two * coeff_two
    miss = jnp.sqrt(miss_a * miss_a + miss_b * miss_b + miss_c * miss_c)
    return (coeff_one, coeff_two, miss)


def finish_kernel(parts_ref, p_ref, q_ref, out_ref, miss_ref):
    (beta, len_one, len_two), (cos_01, cos_02, cos_12) = merge(parts_ref[...])
    rel_one = len_one / beta
    proj_one = rel_one * cos_01
    sine_sq = 1.0 - cos_01 * cos_01
    sub_one = rel_one * jnp.sqrt(sine_sq)
    rel_two = len_two / beta / sub_one
    proj_two_a = rel_two * cos_02 - proj_one * (proj_one / sub_one)
    side = (cos_12 - cos_01 * cos_02) / jnp.sqrt(sine_sq)
    proj_two_b = rel_two * side - proj_one
    sub_two = rel_two * jnp.sqrt(1.0 - cos_02 * cos_02 - side * side)
    coeff_one, coeff_two, miss = least_squares(beta, proj_one, sub_one, proj_two_a, proj_two_b, sub_two)
    miss_ref[...] = miss
    second = coeff_two / sub_one
    first = (coeff_one - second * proj_one) / beta
    out_ref[...] = first * p_ref[...] + (second / beta) * q_ref[...]


def shape(*dims, kind=f32):
    return jax.ShapeDtypeStruct(dims, kind)


VMEM = pl.BlockSpec(memory_space=pltpu.VMEM)
SMEM = pl.BlockSpec(memory_space=pltpu.SMEM)
HBM = pl.BlockSpec(memory_space=pltpu.HBM)


def call(name, kernel, out_shape, scalars, operands, place=VMEM, flops=0, scratch=(), out_place=None):
    size = sum(4 * a.size for a in operands)
    return pl.pallas_call(
        kernel,
        out_shape=out_shape,
        in_specs=[SMEM] * len(scalars) + [place] * len(operands),
        scratch_shapes=scratch,
        **({} if out_place is None else {"out_specs": out_place}),
        compiler_params=pltpu.CompilerParams(vmem_limit_bytes=LIMIT),
        cost_estimate=pl.CostEstimate(flops=flops, bytes_accessed=size, transcendentals=0),
        name=name,
    )(*scalars, *operands)


def body(mesh, rhs, blocks, coupling, inverse, deflation, counts, panel, intersection_rows):
    source, mats, couple, inv = rhs[0, 0], blocks[0, 0], coupling[0, 0], inverse[0, 0]
    defl, panel_mat = deflation[0, 0], panel[0]
    idx = intersection_rows[0]
    many = idx.shape[1]
    half = many // 2
    nrows, ncols = source.shape
    kmax = defl.shape[0]
    n_sub, n_blk = mesh.shape["sub"], mesh.shape["blk"]
    odd = jnp.bitwise_and(lax.axis_index("sub").astype(jnp.int32), 1)[None]
    slot = lax.axis_index("blk").astype(jnp.int32)[None]
    near_pairs = [(i, i ^ 1) for i in range(n_sub) if i ^ 1 < n_sub]
    far_pairs = [(i, ((i + 1) ^ 1) - 1) for i in range(1, n_sub) if ((i + 1) ^ 1) - 1 < n_sub]

    def halo(far, near):
        far = lax.ppermute(far, "sub", far_pairs)
        return far, lax.ppermute(near, "sub", near_pairs)

    def precond(vector, sent, got, coef):
        coefs = lax.all_to_all(coef, "blk", 0, 0)
        *parts, far, near = call(
            "local_solve", local_kernel,
            (
                shape(nrows, ncols), shape(many, ncols), shape(WIDE, ncols, kind=bf16), shape(half, ncols),
                shape(half, ncols),
            ),
            (odd, slot), (vector, *sent, *got, *inv_halves, inv, coefs, panel_mat, lift, gather),
            flops=10**9,
        )
        return parts, (far, near)

    lines = -(-kmax // 16) * 16
    *sent, coef, source, inv, gather, scatter, zrows, lift, off = call(
        "first_rows", prep_kernel,
        (
            shape(3 * half, ncols), shape(3 * half, ncols), shape(n_blk, kmax, ncols), shape(nrows, ncols),
            shape(*inv.shape), shape(many + 2 * lines, nrows, kind=bf16), shape(nrows, many + WIDE, kind=bf16),
            shape(2 * lines, many, kind=bf16), shape(many, WIDE, kind=bf16), shape(nrows, 128),
        ),
        (counts, odd, slot), [pltpu.with_memory_space_constraint(a, pltpu.HBM) for a in (source, idx, defl, inv)],
        place=HBM, flops=3 * 10**8, out_place=[VMEM] * 10,
        scratch=(pltpu.VMEM(idx.shape, jnp.int32), pltpu.VMEM(defl.shape, f32), pltpu.SemaphoreType.DMA((9,))),
    )
    got = inv_halves = halo(*sent)
    parts, halves = precond(source, sent, got, coef)
    z_got = halo(*halves)
    search_one, diag, diag_rows, diag_coef = call(
        "block_product", blocks_kernel,
        (shape(nrows, ncols), shape(nrows, ncols), shape(many, ncols), shape(lines, ncols)),
        (), (*parts, mats, scatter, gather), flops=10**9,
    )
    image, *sent_two, coef, image_rows = call(
        "image", image_kernel,
        (
            shape(nrows, ncols), shape(many, ncols), shape(many, ncols), shape(n_blk, kmax, ncols),
            shape(many, ncols),
        ),
        (odd,), (diag, diag_rows, diag_coef, zrows, couple, *z_got, scatter), flops=5 * 10**8,
    )
    got = halo(*sent_two)
    parts, halves = precond(image, sent_two, got, coef)
    z_got = halo(*halves)
    search_two, diag_rows, unit_one, unit_two, sums = call(
        "last_block_product", last_blocks_kernel,
        (shape(nrows, ncols), shape(many, ncols), shape(many, ncols), shape(many, ncols), shape(8, ncols)),
        (), (*parts, mats, scatter, gather, off, source, image, *sent, image_rows), flops=10**9,
        scratch=(pltpu.VMEM(source.shape, f32),),
    )
    plane, depth = sum_groups(mesh)
    parts = call(
        "lengths_cosines", gram_kernel, shape(len(plane[0]), 8, ncols),
        (odd,), (diag_rows, couple, *z_got, unit_one, unit_two, sums), flops=2 * 10**8,
    )
    parts = lax.all_to_all(parts, AXES, 0, 0, axis_index_groups=plane)
    parts = call("merge_plane", merge_kernel, shape(len(depth[0]), 8, ncols), (), (parts,))
    parts = lax.all_to_all(parts, AXES, 0, 0, axis_index_groups=depth)
    answer, miss = call(
        "combine", finish_kernel, (shape(nrows, ncols), shape(1, ncols)), (), (parts, search_one, search_two),
    )
    return (answer[None, None], miss[0])


def sum_groups(mesh):
    n_sub, n_blk = mesh.shape["sub"], mesh.shape["blk"]
    near = min(8, n_sub)
    size = near * n_blk
    count = n_sub // near
    plane = [[g * size + k for k in range(size)] for g in range(count)]
    depth = [[g * size + k for g in range(count)] for k in range(size)]
    return plane, depth


def solution(mesh):
    placed = (
        P("sub", "blk", None, None),
        P("sub", "blk", None, None, None),
        P("sub", "blk", None, None, None),
        P("sub", "blk", None, None, None),
        P("sub", "blk", None, None),
        P("sub", "blk"),
        P("sub", None, None),
        P("sub", "blk", None),
    )
    return jax.shard_map(
        functools.partial(body, mesh),
        mesh=mesh,
        in_specs=placed,
        out_specs=(P("sub", "blk", None, None), P()),
        check_vma=False,
    )
```

```python
import functools

import jax
import jax.numpy as jnp
from jax import lax
from jax.experimental import pallas as pl
from jax.experimental.pallas import tpu as pltpu
from jax.sharding import PartitionSpec as P

f32 = jnp.float32
bf16 = jnp.bfloat16
AXES = ("sub", "blk")
WIDE = 128
LIMIT = 24 * 1024 * 1024


def split(a):
    high = a.astype(bf16)
    return high, (a - high.astype(f32)).astype(bf16)


def dot(a, b, dims=((1,), (0,))):
    return lax.dot_general(a, b, (dims, ((), ())), preferred_element_type=f32)


def mul(a, b, dims=((1,), (0,))):
    return dot(a[0], b[0], dims) + (dot(a[0], b[1], dims) + dot(a[1], b[0], dims))


def pick(onehot, b):
    return dot(onehot, b[0]) + dot(onehot, b[1])


def gather_matrix(idx, nrows):
    count = idx.shape[1]
    column = jnp.broadcast_to(idx.astype(f32), (128, count)).T
    lane = lax.broadcasted_iota(jnp.int32, (count, 128), 1).astype(f32)
    parts = [
        jnp.where(column == lane + float(128 * k), 1.0, 0.0).astype(bf16)
        for k in range(nrows // 128)
    ]
    return jnp.concatenate(parts, axis=1)


def scatter_matrix(idx, nrows):
    row = lax.broadcasted_iota(jnp.int32, (nrows, idx.shape[1]), 0)
    return jnp.where(row == idx, 1.0, 0.0).astype(bf16)


def masked_deflation(defl, count):
    row = lax.broadcasted_iota(jnp.int32, defl.shape, 0)
    return jnp.where(row < count, defl, 0.0)


def edge_block(high, ref, width):
    start = pl.multiple_of(jnp.where(high, ref.shape[0] - width, 0), width)
    return ref[pl.ds(start, width)]


def padded(a, count):
    return jnp.concatenate([a, jnp.zeros((count - a.shape[0], a.shape[1]), a.dtype)], 0)


def tripled(high, low):
    return padded(jnp.concatenate([high, high, low], 0), WIDE).astype(bf16)


def gather_all(gather_ref, many, lines, a):
    high, low = split(a)
    top = dot(gather_ref[...], high)
    rest = dot(gather_ref[: many + lines], low)
    return top[:many] + rest[:many], top[many : many + lines] + (top[many + lines :] + rest[many:])


def prep_kernel(
    count_ref, odd_ref, slot_ref, r_hbm, idx_hbm, defl_hbm, inv_hbm,
    far_ref, near_ref, coef_ref, r_ref, inv_ref, gather_ref, scatter_ref, zrows_ref, lift_ref, off_ref,
    idx_ref, defl_ref, sems,
):
    many = idx_ref.shape[1]
    half = many // 2
    nrows, ncols = r_ref.shape
    kmax = defl_ref.shape[0]
    lines = zrows_ref.shape[0] // 2
    step = nrows // 4
    blocks, width = inv_ref.shape[0], inv_ref.shape[2]
    odd = odd_ref[0] == 1
    pieces = [(idx_hbm, idx_ref), (defl_hbm, defl_ref)]
    pieces += [(r_hbm.at[pl.ds(k * step, step)], r_ref.at[pl.ds(k * step, step)]) for k in range(4)]
    pieces += [(inv_hbm.at[k], inv_ref.at[k]) for k in (0, blocks - 1)]
    pieces += [(inv_hbm.at[pl.ds(1, blocks - 2)], inv_ref.at[pl.ds(1, blocks - 2)])]
    copies = [pltpu.make_async_copy(a, b, sems.at[k]) for k, (a, b) in enumerate(pieces)]
    for copy in copies:
        copy.start()
    copies[0].wait()
    low, high = idx_ref[:, :half], idx_ref[:, half:]
    idx = jnp.concatenate([jnp.where(odd, low, high), jnp.where(odd, high, low)], 1)
    gather = gather_matrix(idx, nrows)
    scatter = scatter_matrix(idx, nrows)
    gather_ref[:many] = gather
    scatter_ref[:, :many] = scatter
    off_ref[...] = 1.0 - dot(scatter, jnp.ones((many, off_ref.shape[1]), bf16))
    copies[1].wait()
    masked = masked_deflation(defl_ref[...], count_ref[0, 0])
    z_high = masked.astype(bf16).astype(f32)
    z_low = (masked - z_high).astype(bf16).astype(f32)
    z_pair = jnp.concatenate([padded(z_high, lines), padded(z_low, lines)], 0).astype(bf16)
    gather_ref[many:] = z_pair
    zrows_ref[...] = dot(z_pair, scatter).astype(bf16)
    lift = padded(jnp.concatenate([z_high, z_low, z_high], 0), WIDE).T.astype(bf16)
    scatter_ref[:, many:] = lift
    lift_ref[...] = dot(gather, lift).astype(bf16)
    for copy in copies[2:6]:
        copy.wait()
    rows, coef = gather_all(gather_ref, many, lines, r_ref[...])
    for k in range(coef_ref.shape[0]):
        coef_ref[k] = coef[:kmax]
    copies[6].wait()
    copies[7].wait()
    for k, (ref, high) in enumerate(((near_ref, odd_ref[0] == 0), (far_ref, odd))):
        ref[:half] = rows[k * half : (k + 1) * half]
        ref[half : 2 * half] = edge_block(high, r_ref, half)
        first, last = inv_ref[0, :half], inv_ref[blocks - 1, width - half :]
        ref[2 * half :, :half] = jnp.where(high, last[:, half:], first[:, :half])
        ref[2 * half :, half:] = jnp.where(high, last[:, :half], first[:, half:])
    copies[8].wait()


def local_kernel(
    odd_ref, slot_ref, r_ref, far_ref, near_ref, gfar_ref, gnear_ref, inv_far_ref, inv_near_ref,
    inv_ref, all_ref, panel_ref, lift_ref, gather_ref, own_ref, back_ref, coarse_ref, zfar_ref, znear_ref,
):
    odd = odd_ref[0] == 1
    half = znear_ref.shape[0]
    nrows, ncols = r_ref.shape
    kmax = all_ref.shape[1]
    width = inv_ref.shape[1]
    last = inv_ref.shape[0] - 1
    slot = pl.multiple_of(slot_ref[0] * kmax, 8)
    panel = split(panel_ref[pl.ds(slot, kmax), :])
    coefs = split(all_ref[...].reshape(all_ref.shape[0] * kmax, ncols))
    coarse = mul(panel, coefs)
    high = coarse.astype(bf16).astype(f32)
    coarse = tripled(high, coarse - high)
    coarse_ref[...] = coarse
    rows = dot(lift_ref[...], coarse)
    got_lo = jnp.where(odd, gnear_ref[:half], gfar_ref[:half])
    got_hi = jnp.where(odd, gfar_ref[:half], gnear_ref[:half])
    for n in range(last + 1):
        low = half if n == 0 else 0
        high = width - half if n == last else width
        if n == 0:
            part = jnp.concatenate([got_lo, r_ref[:half]], 0)
        elif n == last:
            part = jnp.concatenate([r_ref[nrows - half :], got_hi], 0)
        else:
            part = r_ref[n * width - half : (n + 1) * width - half]
        at = slice(n * width + low - half, n * width + high - half)
        y = mul(split(inv_ref[n, low:high]), split(part))
        own_ref[at] = y
        rows = rows + pick(gather_ref[: 2 * half, at], split(y))
    back = [
        mul(split(inverse[2 * half :]), split(jnp.concatenate([own[:half], got[half : 2 * half]], 0)))
        for own, got, inverse in ((near_ref, gnear_ref, inv_near_ref), (far_ref, gfar_ref, inv_far_ref))
    ]
    back = jnp.concatenate(back, 0)
    back_ref[...] = back
    rows = rows + back
    znear_ref[...] = rows[:half]
    zfar_ref[...] = rows[half:]


def block_products(own_ref, back_ref, coarse_ref, mats_ref, scatter_ref, z_ref, t_ref):
    many = back_ref.shape[0]
    high, low = split(back_ref[...])
    width = mats_ref.shape[1]
    both = jnp.concatenate([high, coarse_ref[...]], 0)
    for n in range(mats_ref.shape[0]):
        part = slice(n * width, (n + 1) * width)
        z = own_ref[part] + (dot(scatter_ref[part], both) + dot(scatter_ref[part, :many], low))
        z_ref[part] = z
        t_ref[part] = mul(split(mats_ref[n]), split(z))


def blocks_kernel(
    own_ref, back_ref, coarse_ref, mats_ref, scatter_ref, gather_ref, z_ref, t_ref, rows_ref, coef_ref
):
    block_products(own_ref, back_ref, coarse_ref, mats_ref, scatter_ref, z_ref, t_ref)
    rows_ref[...], coef = gather_all(gather_ref, rows_ref.shape[0], coef_ref.shape[0], t_ref[...])
    coef_ref[...] = coef


def shared_rows(odd_ref, couple_ref, gfar_ref, gnear_ref):
    near = mul(split(couple_ref[1 - odd_ref[0]]), split(gnear_ref[...]))
    far = mul(split(couple_ref[odd_ref[0]]), split(gfar_ref[...]))
    return jnp.concatenate([near, far], 0)


def image_kernel(
    odd_ref, t_ref, rows_ref, tcoef_ref, zrows_ref, couple_ref, gfar_ref, gnear_ref, scatter_ref,
    u_ref, far_ref, near_ref, coef_ref, urows_ref,
):
    add = shared_rows(odd_ref, couple_ref, gfar_ref, gnear_ref)
    many = add.shape[0]
    half = many // 2
    lines = tcoef_ref.shape[0]
    rows = rows_ref[...] + add
    urows_ref[...] = rows
    high, low = split(add)
    u_ref[...] = t_ref[...] + (dot(scatter_ref[:, :many], high) + dot(scatter_ref[:, :many], low))
    near_ref[:half] = rows[:half]
    far_ref[:half] = rows[half:]
    near_ref[half:] = edge_block(odd_ref[0] == 0, u_ref, half)
    far_ref[half:] = edge_block(odd_ref[0] == 1, u_ref, half)
    coef = dot(zrows_ref[...], high)
    coef = tcoef_ref[...] + (coef[:lines] + (coef[lines:] + dot(zrows_ref[:lines], low)))
    for k in range(coef_ref.shape[0]):
        coef_ref[k] = coef[: coef_ref.shape[1]]


def inverse_or_zero(a):
    return jnp.where(a > 0.0, 1.0 / jnp.where(a > 0.0, a, 1.0), 0.0)


def total(a):
    return jnp.sum(a, axis=0, keepdims=True)


PAIRS = ((0, 1), (0, 2), (1, 2))


def stacked(rows):
    return jnp.concatenate(rows + [jnp.zeros_like(rows[0])] * (8 - len(rows)), 0)


def last_blocks_kernel(
    own_ref, back_ref, coarse_ref, mats_ref, scatter_ref, gather_ref, off_ref,
    u0_ref, u1_ref, far0_ref, near0_ref, rows1_ref,
    z_ref, rows_ref, unit0_ref, unit1_ref, sums_ref, t_ref,
):
    many, ncols = rows_ref.shape
    half = many // 2
    nrows = z_ref.shape[0]
    lanes = off_ref.shape[1]
    block_products(own_ref, back_ref, coarse_ref, mats_ref, scatter_ref, z_ref, t_ref)
    rows_ref[...] = pick(gather_ref[:many], split(t_ref[...]))
    for at in range(0, nrows, 8):
        keep = off_ref[at : at + 8]
        for col in range(0, ncols, lanes):
            t_ref[at : at + 8, col : col + lanes] *= keep
    tops, factors = [], []
    for ref in (u0_ref, u1_ref, t_ref):
        top = jnp.max(jnp.abs(ref[...]).reshape(nrows // 8, 8, ncols), axis=0)
        top = jnp.max(top, axis=0, keepdims=True)
        tops.append(top)
        factors.append(inverse_or_zero(top))
    pairs = ((0, 0), (1, 1), (0, 1), (2, 2), (0, 2), (1, 2))
    sums = [jnp.zeros((8, ncols), f32)] * len(pairs)
    for at in range(0, nrows, 8):
        now = [ref[at : at + 8] * factor for ref, factor in zip((u0_ref, u1_ref, t_ref), factors)]
        sums = [total_ + now[i] * now[j] for total_, (i, j) in zip(sums, pairs)]
    sum_00, sum_11, sum_01, sum_22, sum_02, sum_12 = (total(a) for a in sums)
    size0, size1 = jnp.sqrt(sum_00), jnp.sqrt(sum_11)
    shrink0, shrink1 = inverse_or_zero(size0), inverse_or_zero(size1)
    unit0_ref[:half] = near0_ref[:half] * factors[0] * shrink0
    unit0_ref[half:] = far0_ref[:half] * factors[0] * shrink0
    unit1_ref[...] = rows1_ref[...] * factors[1] * shrink1
    sums_ref[...] = stacked(
        [
            tops[0] * size0, tops[1] * size1, tops[2], sum_01 * shrink0 * shrink1,
            sum_22, sum_02 * shrink0, sum_12 * shrink1,
        ]
    )


def gram_kernel(odd_ref, rows_ref, couple_ref, gfar_ref, gnear_ref, unit0_ref, unit1_ref, sums_ref, out_ref):
    rows = rows_ref[...] + shared_rows(odd_ref, couple_ref, gfar_ref, gnear_ref)
    len0, len1, top_off, cos_01, sum_22, sum_02, sum_12 = (sums_ref[k : k + 1] for k in range(7))
    top = jnp.maximum(top_off, jnp.max(jnp.abs(rows), axis=0, keepdims=True))
    scale = inverse_or_zero(top)
    rows = rows * scale
    ratio = top_off * scale
    size = jnp.sqrt(sum_22 * (ratio * ratio) + total(rows * rows))
    shrink = inverse_or_zero(size)
    cos_02 = (sum_02 * ratio + total(unit0_ref[...] * rows)) * shrink
    cos_12 = (sum_12 * ratio + total(unit1_ref[...] * rows)) * shrink
    send_packed([len0, len1, top * size, cos_01, cos_02, cos_12], out_ref)


def merge(parts):
    lengths, shares = [], []
    for own in parts[:3]:
        top = jnp.max(own, axis=0, keepdims=True)
        share = own * inverse_or_zero(top)
        size = jnp.sqrt(total(share * share))
        lengths.append(top * size)
        shares.append(share * inverse_or_zero(size))
    cosines = [
        total(parts[3 + k] * shares[i] * shares[j])
        for k, (i, j) in enumerate(PAIRS)
    ]
    return lengths, cosines


def unpacked(ref):
    ncols = ref.shape[2] // 6
    return [ref[:, 0, k * ncols : (k + 1) * ncols] for k in range(6)]


def send_packed(rows, ref):
    full = jnp.concatenate(rows, 1)
    for k in range(ref.shape[0]):
        ref[k] = full


def merge_kernel(parts_ref, out_ref):
    lengths, cosines = merge(unpacked(parts_ref))
    send_packed(lengths + cosines, out_ref)


def least_squares(beta, proj_one, sub_one, proj_two_a, proj_two_b, sub_two):
    diag_one = jnp.sqrt(proj_one * proj_one + sub_one * sub_one)
    cross = (proj_one * proj_two_a + sub_one * proj_two_b) / diag_one
    rest_a = proj_two_a - cross * proj_one / diag_one
    rest_b = proj_two_b - cross * sub_one / diag_one
    diag_two = jnp.sqrt(rest_a * rest_a + rest_b * rest_b + sub_two * sub_two)
    coeff_two = beta * rest_a / (diag_two * diag_two)
    coeff_one = (beta * proj_one / diag_one - cross * coeff_two) / diag_one
    miss_a = beta - proj_one * coeff_one - proj_two_a * coeff_two
    miss_b = sub_one * coeff_one + proj_two_b * coeff_two
    miss_c = sub_two * coeff_two
    miss = jnp.sqrt(miss_a * miss_a + miss_b * miss_b + miss_c * miss_c)
    return (coeff_one, coeff_two, miss)


def finish_kernel(parts_ref, p_ref, q_ref, out_ref, miss_ref):
    (beta, len_one, len_two), (cos_01, cos_02, cos_12) = merge(unpacked(parts_ref))
    rel_one = len_one / beta
    proj_one = rel_one * cos_01
    sine_sq = 1.0 - cos_01 * cos_01
    sub_one = rel_one * jnp.sqrt(sine_sq)
    rel_two = len_two / beta / sub_one
    proj_two_a = rel_two * cos_02 - proj_one * (proj_one / sub_one)
    side = (cos_12 - cos_01 * cos_02) / jnp.sqrt(sine_sq)
    proj_two_b = rel_two * side - proj_one
    sub_two = rel_two * jnp.sqrt(1.0 - cos_02 * cos_02 - side * side)
    coeff_one, coeff_two, miss = least_squares(beta, proj_one, sub_one, proj_two_a, proj_two_b, sub_two)
    miss_ref[...] = miss
    second = coeff_two / sub_one
    first = (coeff_one - second * proj_one) / beta
    out_ref[...] = first * p_ref[...] + (second / beta) * q_ref[...]


def shape(*dims, kind=f32):
    return jax.ShapeDtypeStruct(dims, kind)


VMEM = pl.BlockSpec(memory_space=pltpu.VMEM)
SMEM = pl.BlockSpec(memory_space=pltpu.SMEM)
HBM = pl.BlockSpec(memory_space=pltpu.HBM)


def call(name, kernel, out_shape, scalars, operands, place=VMEM, flops=0, scratch=(), out_place=None):
    size = sum(4 * a.size for a in operands)
    return pl.pallas_call(
        kernel,
        out_shape=out_shape,
        in_specs=[SMEM] * len(scalars) + [place] * len(operands),
        scratch_shapes=scratch,
        **({} if out_place is None else {"out_specs": out_place}),
        compiler_params=pltpu.CompilerParams(vmem_limit_bytes=LIMIT),
        cost_estimate=pl.CostEstimate(flops=flops, bytes_accessed=size, transcendentals=0),
        name=name,
    )(*scalars, *operands)


def body(mesh, rhs, blocks, coupling, inverse, deflation, counts, panel, intersection_rows):
    source, mats, couple, inv = rhs[0, 0], blocks[0, 0], coupling[0, 0], inverse[0, 0]
    defl, panel_mat = deflation[0, 0], panel[0]
    idx = intersection_rows[0]
    many = idx.shape[1]
    half = many // 2
    nrows, ncols = source.shape
    kmax = defl.shape[0]
    n_sub, n_blk = mesh.shape["sub"], mesh.shape["blk"]
    odd = jnp.bitwise_and(lax.axis_index("sub").astype(jnp.int32), 1)[None]
    slot = lax.axis_index("blk").astype(jnp.int32)[None]
    near_pairs = [(i, i ^ 1) for i in range(n_sub) if i ^ 1 < n_sub]
    far_pairs = [(i, ((i + 1) ^ 1) - 1) for i in range(1, n_sub) if ((i + 1) ^ 1) - 1 < n_sub]

    def halo(far, near):
        far = lax.ppermute(far, "sub", far_pairs)
        return far, lax.ppermute(near, "sub", near_pairs)

    def precond(vector, sent, got, coef):
        coefs = lax.all_to_all(coef, "blk", 0, 0)
        *parts, far, near = call(
            "local_solve", local_kernel,
            (
                shape(nrows, ncols), shape(many, ncols), shape(WIDE, ncols, kind=bf16), shape(half, ncols),
                shape(half, ncols),
            ),
            (odd, slot), (vector, *sent, *got, *inv_halves, inv, coefs, panel_mat, lift, gather),
            flops=10**9,
        )
        return parts, (far, near)

    lines = -(-kmax // 16) * 16
    *sent, coef, source, inv, gather, scatter, zrows, lift, off = call(
        "first_rows", prep_kernel,
        (
            shape(3 * half, ncols), shape(3 * half, ncols), shape(n_blk, kmax, ncols), shape(nrows, ncols),
            shape(*inv.shape), shape(many + 2 * lines, nrows, kind=bf16), shape(nrows, many + WIDE, kind=bf16),
            shape(2 * lines, many, kind=bf16), shape(many, WIDE, kind=bf16), shape(nrows, 128),
        ),
        (counts, odd, slot), [pltpu.with_memory_space_constraint(a, pltpu.HBM) for a in (source, idx, defl, inv)],
        place=HBM, flops=3 * 10**8, out_place=[VMEM] * 10,
        scratch=(pltpu.VMEM(idx.shape, jnp.int32), pltpu.VMEM(defl.shape, f32), pltpu.SemaphoreType.DMA((9,))),
    )
    got = inv_halves = halo(*sent)
    parts, halves = precond(source, sent, got, coef)
    z_got = halo(*halves)
    search_one, diag, diag_rows, diag_coef = call(
        "block_product", blocks_kernel,
        (shape(nrows, ncols), shape(nrows, ncols), shape(many, ncols), shape(lines, ncols)),
        (), (*parts, mats, scatter, gather), flops=10**9,
    )
    image, *sent_two, coef, image_rows = call(
        "image", image_kernel,
        (
            shape(nrows, ncols), shape(many, ncols), shape(many, ncols), shape(n_blk, kmax, ncols),
            shape(many, ncols),
        ),
        (odd,), (diag, diag_rows, diag_coef, zrows, couple, *z_got, scatter), flops=5 * 10**8,
    )
    got = halo(*sent_two)
    parts, halves = precond(image, sent_two, got, coef)
    z_got = halo(*halves)
    search_two, diag_rows, unit_one, unit_two, sums = call(
        "last_block_product", last_blocks_kernel,
        (shape(nrows, ncols), shape(many, ncols), shape(many, ncols), shape(many, ncols), shape(8, ncols)),
        (), (*parts, mats, scatter, gather, off, source, image, *sent, image_rows), flops=10**9,
        scratch=(pltpu.VMEM(source.shape, f32),),
    )
    plane, depth = sum_groups(mesh)
    parts = call(
        "lengths_cosines", gram_kernel, shape(len(plane[0]), 1, 6 * ncols),
        (odd,), (diag_rows, couple, *z_got, unit_one, unit_two, sums), flops=2 * 10**8,
    )
    parts = lax.all_to_all(parts, AXES, 0, 0, axis_index_groups=plane)
    parts = call("merge_plane", merge_kernel, shape(len(depth[0]), 1, 6 * ncols), (), (parts,))
    parts = lax.all_to_all(parts, AXES, 0, 0, axis_index_groups=depth)
    answer, miss = call(
        "combine", finish_kernel, (shape(nrows, ncols), shape(1, ncols)), (), (parts, search_one, search_two),
    )
    return (answer[None, None], miss[0])


def sum_groups(mesh):
    n_sub, n_blk = mesh.shape["sub"], mesh.shape["blk"]
    near = min(8, n_sub)
    size = near * n_blk
    count = n_sub // near
    plane = [[g * size + k for k in range(size)] for g in range(count)]
    depth = [[g * size + k for g in range(count)] for k in range(size)]
    return plane, depth


def solution(mesh):
    placed = (
        P("sub", "blk", None, None),
        P("sub", "blk", None, None, None),
        P("sub", "blk", None, None, None),
        P("sub", "blk", None, None, None),
        P("sub", "blk", None, None),
        P("sub", "blk"),
        P("sub", None, None),
        P("sub", "blk", None),
    )
    return jax.shard_map(
        functools.partial(body, mesh),
        mesh=mesh,
        in_specs=placed,
        out_specs=(P("sub", "blk", None, None), P()),
        check_vma=False,
    )
```

```python
import functools

import jax
import jax.numpy as jnp
from jax import lax
from jax.experimental import pallas as pl
from jax.experimental.pallas import tpu as pltpu
from jax.sharding import PartitionSpec as P

f32 = jnp.float32
bf16 = jnp.bfloat16
AXES = ("sub", "blk")
WIDE = 128
LEAST, MOST = 1e-12, 1e24
LIMIT = 24 * 1024 * 1024


def split(a):
    high = a.astype(bf16)
    return high, (a - high.astype(f32)).astype(bf16)


def dot(a, b, dims=((1,), (0,))):
    return lax.dot_general(a, b, (dims, ((), ())), preferred_element_type=f32)


def mul(a, b, dims=((1,), (0,))):
    return dot(a[0], b[0], dims) + (dot(a[0], b[1], dims) + dot(a[1], b[0], dims))


def pick(onehot, b):
    return dot(onehot, b[0]) + dot(onehot, b[1])


def gather_matrix(idx, nrows):
    count = idx.shape[1]
    column = jnp.broadcast_to(idx.astype(f32), (128, count)).T
    lane = lax.broadcasted_iota(jnp.int32, (count, 128), 1).astype(f32)
    parts = [
        jnp.where(column == lane + float(128 * k), 1.0, 0.0).astype(bf16)
        for k in range(nrows // 128)
    ]
    return jnp.concatenate(parts, axis=1)


def scatter_matrix(idx, nrows):
    row = lax.broadcasted_iota(jnp.int32, (nrows, idx.shape[1]), 0)
    return jnp.where(row == idx, 1.0, 0.0).astype(bf16)


def masked_deflation(defl, count):
    row = lax.broadcasted_iota(jnp.int32, defl.shape, 0)
    return jnp.where(row < count, defl, 0.0)


def edge_block(high, ref, width):
    start = pl.multiple_of(jnp.where(high, ref.shape[0] - width, 0), width)
    return ref[pl.ds(start, width)]


def padded(a, count):
    return jnp.concatenate([a, jnp.zeros((count - a.shape[0], a.shape[1]), a.dtype)], 0)


def tripled(high, low):
    return padded(jnp.concatenate([high, high, low], 0), WIDE).astype(bf16)


def gather_all(gather_ref, many, lines, a):
    high, low = split(a)
    top = dot(gather_ref[...], high)
    rest = dot(gather_ref[: many + lines], low)
    return top[:many] + rest[:many], top[many : many + lines] + (top[many + lines :] + rest[many:])


def prep_kernel(
    count_ref, odd_ref, slot_ref, r_hbm, idx_hbm, defl_hbm, inv_hbm,
    far_ref, near_ref, coef_ref, r_ref, inv_ref, gather_ref, scatter_ref, zrows_ref, lift_ref, off_ref,
    idx_ref, defl_ref, sems,
):
    many = idx_ref.shape[1]
    half = many // 2
    nrows, ncols = r_ref.shape
    kmax = defl_ref.shape[0]
    lines = zrows_ref.shape[0] // 2
    step = nrows // 4
    blocks, width = inv_ref.shape[0], inv_ref.shape[2]
    odd = odd_ref[0] == 1
    pieces = [(idx_hbm, idx_ref), (defl_hbm, defl_ref)]
    pieces += [(r_hbm.at[pl.ds(k * step, step)], r_ref.at[pl.ds(k * step, step)]) for k in range(4)]
    pieces += [(inv_hbm.at[k], inv_ref.at[k]) for k in (0, blocks - 1)]
    pieces += [(inv_hbm.at[pl.ds(1, blocks - 2)], inv_ref.at[pl.ds(1, blocks - 2)])]
    copies = [pltpu.make_async_copy(a, b, sems.at[k]) for k, (a, b) in enumerate(pieces)]
    for copy in copies:
        copy.start()
    copies[0].wait()
    low, high = idx_ref[:, :half], idx_ref[:, half:]
    idx = jnp.concatenate([jnp.where(odd, low, high), jnp.where(odd, high, low)], 1)
    gather = gather_matrix(idx, nrows)
    scatter = scatter_matrix(idx, nrows)
    gather_ref[:many] = gather
    scatter_ref[:, :many] = scatter
    off_ref[...] = 1.0 - dot(scatter, jnp.ones((many, off_ref.shape[1]), bf16))
    copies[1].wait()
    masked = masked_deflation(defl_ref[...], count_ref[0, 0])
    z_high = masked.astype(bf16).astype(f32)
    z_low = (masked - z_high).astype(bf16).astype(f32)
    z_pair = jnp.concatenate([padded(z_high, lines), padded(z_low, lines)], 0).astype(bf16)
    gather_ref[many:] = z_pair
    zrows_ref[...] = dot(z_pair, scatter).astype(bf16)
    lift = padded(jnp.concatenate([z_high, z_low, z_high], 0), WIDE).T.astype(bf16)
    scatter_ref[:, many:] = lift
    lift_ref[...] = dot(gather, lift).astype(bf16)
    for copy in copies[2:6]:
        copy.wait()
    rows, coef = gather_all(gather_ref, many, lines, r_ref[...])
    for k in range(coef_ref.shape[0]):
        coef_ref[k] = coef[:kmax]
    copies[6].wait()
    copies[7].wait()
    for k, (ref, high) in enumerate(((near_ref, odd_ref[0] == 0), (far_ref, odd))):
        ref[:half] = rows[k * half : (k + 1) * half]
        ref[half : 2 * half] = edge_block(high, r_ref, half)
        first, last = inv_ref[0, :half], inv_ref[blocks - 1, width - half :]
        ref[2 * half :, :half] = jnp.where(high, last[:, half:], first[:, :half])
        ref[2 * half :, half:] = jnp.where(high, last[:, :half], first[:, half:])
    copies[8].wait()


def local_kernel(
    odd_ref, slot_ref, r_ref, far_ref, near_ref, gfar_ref, gnear_ref, inv_far_ref, inv_near_ref,
    inv_ref, all_ref, panel_ref, lift_ref, gather_ref, own_ref, back_ref, coarse_ref, zfar_ref, znear_ref,
):
    odd = odd_ref[0] == 1
    half = znear_ref.shape[0]
    nrows, ncols = r_ref.shape
    kmax = all_ref.shape[1]
    width = inv_ref.shape[1]
    last = inv_ref.shape[0] - 1
    slot = pl.multiple_of(slot_ref[0] * kmax, 8)
    panel = split(panel_ref[pl.ds(slot, kmax), :])
    coefs = split(all_ref[...].reshape(all_ref.shape[0] * kmax, ncols))
    coarse = mul(panel, coefs)
    high = coarse.astype(bf16).astype(f32)
    coarse = tripled(high, coarse - high)
    coarse_ref[...] = coarse
    rows = dot(lift_ref[...], coarse)
    got_lo = jnp.where(odd, gnear_ref[:half], gfar_ref[:half])
    got_hi = jnp.where(odd, gfar_ref[:half], gnear_ref[:half])
    for n in range(last + 1):
        low = half if n == 0 else 0
        high = width - half if n == last else width
        if n == 0:
            part = jnp.concatenate([got_lo, r_ref[:half]], 0)
        elif n == last:
            part = jnp.concatenate([r_ref[nrows - half :], got_hi], 0)
        else:
            part = r_ref[n * width - half : (n + 1) * width - half]
        at = slice(n * width + low - half, n * width + high - half)
        y = mul(split(inv_ref[n, low:high]), split(part))
        own_ref[at] = y
        rows = rows + pick(gather_ref[: 2 * half, at], split(y))
    back = [
        mul(split(inverse[2 * half :]), split(jnp.concatenate([own[:half], got[half : 2 * half]], 0)))
        for own, got, inverse in ((near_ref, gnear_ref, inv_near_ref), (far_ref, gfar_ref, inv_far_ref))
    ]
    back = jnp.concatenate(back, 0)
    back_ref[...] = back
    rows = rows + back
    znear_ref[...] = rows[:half]
    zfar_ref[...] = rows[half:]


def block_products(own_ref, back_ref, coarse_ref, mats_ref, scatter_ref, z_ref, t_ref):
    many = back_ref.shape[0]
    high, low = split(back_ref[...])
    width = mats_ref.shape[1]
    both = jnp.concatenate([high, coarse_ref[...]], 0)
    for n in range(mats_ref.shape[0]):
        part = slice(n * width, (n + 1) * width)
        z = own_ref[part] + (dot(scatter_ref[part], both) + dot(scatter_ref[part, :many], low))
        z_ref[part] = z
        t_ref[part] = mul(split(mats_ref[n]), split(z))


def blocks_kernel(
    own_ref, back_ref, coarse_ref, mats_ref, scatter_ref, gather_ref, z_ref, t_ref, rows_ref, coef_ref
):
    block_products(own_ref, back_ref, coarse_ref, mats_ref, scatter_ref, z_ref, t_ref)
    rows_ref[...], coef = gather_all(gather_ref, rows_ref.shape[0], coef_ref.shape[0], t_ref[...])
    coef_ref[...] = coef


def shared_rows(odd_ref, couple_ref, gfar_ref, gnear_ref):
    near = mul(split(couple_ref[1 - odd_ref[0]]), split(gnear_ref[...]))
    far = mul(split(couple_ref[odd_ref[0]]), split(gfar_ref[...]))
    return jnp.concatenate([near, far], 0)


def image_kernel(
    odd_ref, t_ref, rows_ref, tcoef_ref, zrows_ref, couple_ref, gfar_ref, gnear_ref, scatter_ref,
    u_ref, far_ref, near_ref, coef_ref, urows_ref,
):
    add = shared_rows(odd_ref, couple_ref, gfar_ref, gnear_ref)
    many = add.shape[0]
    half = many // 2
    lines = tcoef_ref.shape[0]
    rows = rows_ref[...] + add
    urows_ref[...] = rows
    high, low = split(add)
    u_ref[...] = t_ref[...] + (dot(scatter_ref[:, :many], high) + dot(scatter_ref[:, :many], low))
    near_ref[:half] = rows[:half]
    far_ref[:half] = rows[half:]
    near_ref[half:] = edge_block(odd_ref[0] == 0, u_ref, half)
    far_ref[half:] = edge_block(odd_ref[0] == 1, u_ref, half)
    coef = dot(zrows_ref[...], high)
    coef = tcoef_ref[...] + (coef[:lines] + (coef[lines:] + dot(zrows_ref[:lines], low)))
    for k in range(coef_ref.shape[0]):
        coef_ref[k] = coef[: coef_ref.shape[1]]


highest = lax.Precision.HIGHEST


def with_halo(array, sides, width):
    for axis, dim in sides:
        peers, length = (lax.axis_size(axis), array.shape[dim])
        up = [(i, (i + 1) % peers) for i in range(peers - 1)]
        down = [(j, i) for i, j in up]
        last = lax.slice_in_dim(array, length - width, length, axis=dim)
        first = lax.slice_in_dim(array, 0, width, axis=dim)
        before = lax.ppermute(last, axis, up)
        after = lax.ppermute(first, axis, down)
        array = jnp.concatenate([before, array, after], axis=dim)
    return array


def apply_operator(field, block_mats, couple, low_idx, high_idx):
    half = low_idx.shape[0]
    sent = jnp.concatenate([field[low_idx], field[high_idx]], 0)
    padded = with_halo(sent, (("sub", 0),), half)
    from_low = padded[:half]
    from_high = padded[padded.shape[0] - half :]
    count_blocks, width = (block_mats.shape[0], block_mats.shape[1])
    local = jnp.einsum(
        "nij,njr->nir",
        block_mats,
        field.reshape(count_blocks, width, field.shape[1]),
        precision=highest,
    )
    local = local.reshape(field.shape)
    local = local.at[low_idx].add(jnp.dot(couple[0], from_low, precision=highest))
    return local.at[high_idx].add(jnp.dot(couple[1], from_high, precision=highest))


def apply_precond(resid, inv_mats, masked, panel_mat, low_idx, high_idx):
    half = low_idx.shape[0]
    nrows, ncols = resid.shape
    sent = jnp.concatenate([resid[low_idx], resid[high_idx]], 0)
    padded = with_halo(sent, (("sub", 0),), half)
    extended = jnp.concatenate([padded[:half], resid, padded[padded.shape[0] - half :]], 0)
    count_blocks, width = (inv_mats.shape[0], inv_mats.shape[1])
    solved = jnp.einsum(
        "nij,njr->nir", inv_mats, extended.reshape(count_blocks, width, ncols), precision=highest
    )
    solved = solved.reshape(nrows + 2 * half, ncols)
    own = solved[half : half + nrows]
    back_low = solved[:half]
    back_high = solved[half + nrows :]
    coef = jnp.dot(masked, resid, precision=highest)
    kmax = coef.shape[0]
    slot = lax.axis_index("blk")
    every = lax.all_gather(coef, "blk", axis=0, tiled=True)
    mine = lax.dynamic_slice_in_dim(panel_mat, slot * kmax, kmax, 0)
    correct = jnp.dot(mine, every, precision=highest)
    partial_value = own + jnp.einsum("kn,kr->nr", masked, correct, precision=highest)
    back = jnp.concatenate([back_low, back_high], 0)
    returned = with_halo(back, (("sub", 0),), half)
    field = partial_value.at[low_idx].add(returned[:half])
    field = field.at[high_idx].add(returned[returned.shape[0] - half :])
    return (field, None)


def normalised_solve(rhs, blocks, coupling, inverse, deflation, counts, panel, intersection_rows):
    source = rhs[0, 0]
    block_mats = blocks[0, 0]
    couple = coupling[0, 0]
    inv_mats = inverse[0, 0]
    panel_mat = panel[0]
    index_rows = intersection_rows[0, 0]
    half = index_rows.shape[0] // 2
    low_idx = index_rows[:half]
    high_idx = index_rows[half:]
    kmax = deflation.shape[2]
    keep = (jnp.arange(kmax, dtype=jnp.int32) < counts[0, 0]).astype(jnp.float32)
    masked = deflation[0, 0] * keep[:, None]

    def precond(vector):
        return apply_precond(vector, inv_mats, masked, panel_mat, low_idx, high_idx)

    def operator(vector):
        return apply_operator(vector, block_mats, couple, low_idx, high_idx)

    norm_sq = lax.psum(jnp.sum(source * source, 0), ("sub", "blk"))
    beta = jnp.sqrt(norm_sq)
    basis_one = source / beta
    search_one, rows_one = precond(basis_one)
    image = operator(search_one)
    proj_one, image_sq = lax.psum(
        (jnp.sum(image * basis_one, 0), jnp.sum(image * image, 0)), ("sub", "blk")
    )
    sub_one = jnp.sqrt(image_sq - proj_one * proj_one)
    basis_two = (image - proj_one * basis_one) / sub_one
    search_two, rows_two = precond(basis_two)
    image_two = operator(search_two)
    proj_two_a, proj_two_b, image_two_sq = lax.psum(
        (
            jnp.sum(image_two * basis_one, 0),
            jnp.sum(image_two * basis_two, 0),
            jnp.sum(image_two * image_two, 0),
        ),
        ("sub", "blk"),
    )
    sub_two = jnp.sqrt(image_two_sq - proj_two_a * proj_two_a - proj_two_b * proj_two_b)
    coeff_one, coeff_two, miss = least_squares(
        beta, proj_one, sub_one, proj_two_a, proj_two_b, sub_two
    )
    solution = coeff_one * search_one + coeff_two * search_two
    return (solution, miss)


def inverse_or_zero(a):
    return jnp.where(a > 0.0, 1.0 / jnp.where(a > 0.0, a, 1.0), 0.0)


def total(a):
    return jnp.sum(a, axis=0, keepdims=True)


PAIRS = ((0, 1), (0, 2), (1, 2))


def stacked(rows):
    return jnp.concatenate(rows + [jnp.zeros_like(rows[0])] * (8 - len(rows)), 0)


def last_blocks_kernel(
    own_ref, back_ref, coarse_ref, mats_ref, scatter_ref, gather_ref, off_ref,
    u0_ref, u1_ref, far0_ref, near0_ref, rows1_ref,
    z_ref, rows_ref, unit0_ref, unit1_ref, sums_ref, t_ref,
):
    many, ncols = rows_ref.shape
    half = many // 2
    nrows = z_ref.shape[0]
    lanes = off_ref.shape[1]
    block_products(own_ref, back_ref, coarse_ref, mats_ref, scatter_ref, z_ref, t_ref)
    rows_ref[...] = pick(gather_ref[:many], split(t_ref[...]))
    for at in range(0, nrows, 8):
        keep = off_ref[at : at + 8]
        for col in range(0, ncols, lanes):
            t_ref[at : at + 8, col : col + lanes] *= keep
    tops, factors = [], []
    for ref in (u0_ref, u1_ref, t_ref):
        top = jnp.max(jnp.abs(ref[...]).reshape(nrows // 8, 8, ncols), axis=0)
        top = jnp.max(top, axis=0, keepdims=True)
        tops.append(top)
        factors.append(inverse_or_zero(top))
    pairs = ((0, 0), (1, 1), (0, 1), (2, 2), (0, 2), (1, 2))
    sums = [jnp.zeros((8, ncols), f32)] * len(pairs)
    for at in range(0, nrows, 8):
        now = [ref[at : at + 8] * factor for ref, factor in zip((u0_ref, u1_ref, t_ref), factors)]
        sums = [total_ + now[i] * now[j] for total_, (i, j) in zip(sums, pairs)]
    sum_00, sum_11, sum_01, sum_22, sum_02, sum_12 = (total(a) for a in sums)
    size0, size1 = jnp.sqrt(sum_00), jnp.sqrt(sum_11)
    shrink0, shrink1 = inverse_or_zero(size0), inverse_or_zero(size1)
    unit0_ref[:half] = near0_ref[:half] * factors[0] * shrink0
    unit0_ref[half:] = far0_ref[:half] * factors[0] * shrink0
    unit1_ref[...] = rows1_ref[...] * factors[1] * shrink1
    sums_ref[...] = stacked(
        [
            tops[0] * size0, tops[1] * size1, tops[2], sum_01 * shrink0 * shrink1,
            sum_22, sum_02 * shrink0, sum_12 * shrink1,
        ]
    )


def gram_kernel(odd_ref, rows_ref, couple_ref, gfar_ref, gnear_ref, unit0_ref, unit1_ref, sums_ref, out_ref):
    rows = rows_ref[...] + shared_rows(odd_ref, couple_ref, gfar_ref, gnear_ref)
    len0, len1, top_off, cos_01, sum_22, sum_02, sum_12 = (sums_ref[k : k + 1] for k in range(7))
    top = jnp.maximum(top_off, jnp.max(jnp.abs(rows), axis=0, keepdims=True))
    scale = inverse_or_zero(top)
    rows = rows * scale
    ratio = top_off * scale
    size = jnp.sqrt(sum_22 * (ratio * ratio) + total(rows * rows))
    shrink = inverse_or_zero(size)
    cos_02 = (sum_02 * ratio + total(unit0_ref[...] * rows)) * shrink
    cos_12 = (sum_12 * ratio + total(unit1_ref[...] * rows)) * shrink
    send_packed([len0, len1, top * size, cos_01, cos_02, cos_12], out_ref)


def merge(parts):
    lengths, shares = [], []
    for own in parts[:3]:
        top = jnp.max(own, axis=0, keepdims=True)
        share = own * inverse_or_zero(top)
        size = jnp.sqrt(total(share * share))
        lengths.append(top * size)
        shares.append(share * inverse_or_zero(size))
    cosines = [
        total(parts[3 + k] * shares[i] * shares[j])
        for k, (i, j) in enumerate(PAIRS)
    ]
    return lengths, cosines


def unpacked(ref):
    ncols = ref.shape[2] // 6
    return [ref[:, 0, k * ncols : (k + 1) * ncols] for k in range(6)]


def send_packed(rows, ref):
    full = jnp.concatenate(rows, 1)
    for k in range(ref.shape[0]):
        ref[k] = full


def merge_kernel(parts_ref, out_ref):
    lengths, cosines = merge(unpacked(parts_ref))
    send_packed(lengths + cosines, out_ref)


def least_squares(beta, proj_one, sub_one, proj_two_a, proj_two_b, sub_two):
    diag_one = jnp.sqrt(proj_one * proj_one + sub_one * sub_one)
    cross = (proj_one * proj_two_a + sub_one * proj_two_b) / diag_one
    rest_a = proj_two_a - cross * proj_one / diag_one
    rest_b = proj_two_b - cross * sub_one / diag_one
    diag_two = jnp.sqrt(rest_a * rest_a + rest_b * rest_b + sub_two * sub_two)
    coeff_two = beta * rest_a / (diag_two * diag_two)
    coeff_one = (beta * proj_one / diag_one - cross * coeff_two) / diag_one
    miss_a = beta - proj_one * coeff_one - proj_two_a * coeff_two
    miss_b = sub_one * coeff_one + proj_two_b * coeff_two
    miss_c = sub_two * coeff_two
    miss = jnp.sqrt(miss_a * miss_a + miss_b * miss_b + miss_c * miss_c)
    return (coeff_one, coeff_two, miss)


def judge_kernel(parts_ref, rows_ref, ok_ref):
    (beta, len_one, len_two), (cos_01, cos_02, cos_12) = merge(unpacked(parts_ref))
    rel_one = len_one / beta
    proj_one = rel_one * cos_01
    sine_sq = 1.0 - cos_01 * cos_01
    sub_one = rel_one * jnp.sqrt(sine_sq)
    rel_two = len_two / beta / sub_one
    proj_two_a = rel_two * cos_02 - proj_one * (proj_one / sub_one)
    side = (cos_12 - cos_01 * cos_02) / jnp.sqrt(sine_sq)
    proj_two_b = rel_two * side - proj_one
    sub_two = rel_two * jnp.sqrt(1.0 - cos_02 * cos_02 - side * side)
    coeff_one, coeff_two, miss = least_squares(beta, proj_one, sub_one, proj_two_a, proj_two_b, sub_two)
    second = coeff_two / sub_one
    first = (coeff_one - second * proj_one) / beta
    rows_ref[...] = stacked([first, second / beta, miss])
    good = jnp.where(first * 0.0 + second * 0.0 + miss * 0.0 == 0.0, 1.0, 0.0)
    for a in (beta, len_one, len_two):
        good = jnp.where((a > LEAST) & (a < MOST), good, 0.0)
    ok_ref[0, 0] = jnp.where(jnp.min(good) > 0.0, 1, 0)


def combine_kernel(rows_ref, p_ref, q_ref, out_ref):
    out_ref[...] = rows_ref[0:1] * p_ref[...] + rows_ref[1:2] * q_ref[...]


def shape(*dims, kind=f32):
    return jax.ShapeDtypeStruct(dims, kind)


VMEM = pl.BlockSpec(memory_space=pltpu.VMEM)
SMEM = pl.BlockSpec(memory_space=pltpu.SMEM)
HBM = pl.BlockSpec(memory_space=pltpu.HBM)


def call(name, kernel, out_shape, scalars, operands, place=VMEM, flops=0, scratch=(), out_place=None):
    size = sum(4 * a.size for a in operands)
    return pl.pallas_call(
        kernel,
        out_shape=out_shape,
        in_specs=[SMEM] * len(scalars) + [place] * len(operands),
        scratch_shapes=scratch,
        **({} if out_place is None else {"out_specs": out_place}),
        compiler_params=pltpu.CompilerParams(vmem_limit_bytes=LIMIT),
        cost_estimate=pl.CostEstimate(flops=flops, bytes_accessed=size, transcendentals=0),
        name=name,
    )(*scalars, *operands)


def body(mesh, rhs, blocks, coupling, inverse, deflation, counts, panel, intersection_rows):
    source, mats, couple, inv = rhs[0, 0], blocks[0, 0], coupling[0, 0], inverse[0, 0]
    defl, panel_mat = deflation[0, 0], panel[0]
    idx = intersection_rows[0]
    many = idx.shape[1]
    half = many // 2
    nrows, ncols = source.shape
    kmax = defl.shape[0]
    n_sub, n_blk = mesh.shape["sub"], mesh.shape["blk"]
    odd = jnp.bitwise_and(lax.axis_index("sub").astype(jnp.int32), 1)[None]
    slot = lax.axis_index("blk").astype(jnp.int32)[None]
    near_pairs = [(i, i ^ 1) for i in range(n_sub) if i ^ 1 < n_sub]
    far_pairs = [(i, ((i + 1) ^ 1) - 1) for i in range(1, n_sub) if ((i + 1) ^ 1) - 1 < n_sub]

    def halo(far, near):
        far = lax.ppermute(far, "sub", far_pairs)
        return far, lax.ppermute(near, "sub", near_pairs)

    def precond(vector, sent, got, coef):
        coefs = lax.all_to_all(coef, "blk", 0, 0)
        *parts, far, near = call(
            "local_solve", local_kernel,
            (
                shape(nrows, ncols), shape(many, ncols), shape(WIDE, ncols, kind=bf16), shape(half, ncols),
                shape(half, ncols),
            ),
            (odd, slot), (vector, *sent, *got, *inv_halves, inv, coefs, panel_mat, lift, gather),
            flops=10**9,
        )
        return parts, (far, near)

    lines = -(-kmax // 16) * 16
    *sent, coef, source, inv, gather, scatter, zrows, lift, off = call(
        "first_rows", prep_kernel,
        (
            shape(3 * half, ncols), shape(3 * half, ncols), shape(n_blk, kmax, ncols), shape(nrows, ncols),
            shape(*inv.shape), shape(many + 2 * lines, nrows, kind=bf16), shape(nrows, many + WIDE, kind=bf16),
            shape(2 * lines, many, kind=bf16), shape(many, WIDE, kind=bf16), shape(nrows, 128),
        ),
        (counts, odd, slot), [pltpu.with_memory_space_constraint(a, pltpu.HBM) for a in (source, idx, defl, inv)],
        place=HBM, flops=3 * 10**8, out_place=[VMEM] * 10,
        scratch=(pltpu.VMEM(idx.shape, jnp.int32), pltpu.VMEM(defl.shape, f32), pltpu.SemaphoreType.DMA((9,))),
    )
    got = inv_halves = halo(*sent)
    parts, halves = precond(source, sent, got, coef)
    z_got = halo(*halves)
    search_one, diag, diag_rows, diag_coef = call(
        "block_product", blocks_kernel,
        (shape(nrows, ncols), shape(nrows, ncols), shape(many, ncols), shape(lines, ncols)),
        (), (*parts, mats, scatter, gather), flops=10**9,
    )
    image, *sent_two, coef, image_rows = call(
        "image", image_kernel,
        (
            shape(nrows, ncols), shape(many, ncols), shape(many, ncols), shape(n_blk, kmax, ncols),
            shape(many, ncols),
        ),
        (odd,), (diag, diag_rows, diag_coef, zrows, couple, *z_got, scatter), flops=5 * 10**8,
    )
    got = halo(*sent_two)
    parts, halves = precond(image, sent_two, got, coef)
    z_got = halo(*halves)
    search_two, diag_rows, unit_one, unit_two, sums = call(
        "last_block_product", last_blocks_kernel,
        (shape(nrows, ncols), shape(many, ncols), shape(many, ncols), shape(many, ncols), shape(8, ncols)),
        (), (*parts, mats, scatter, gather, off, source, image, *sent, image_rows), flops=10**9,
        scratch=(pltpu.VMEM(source.shape, f32),),
    )
    plane, depth = sum_groups(mesh)
    parts = call(
        "lengths_cosines", gram_kernel, shape(len(plane[0]), 1, 6 * ncols),
        (odd,), (diag_rows, couple, *z_got, unit_one, unit_two, sums), flops=2 * 10**8,
    )
    parts = lax.all_to_all(parts, AXES, 0, 0, axis_index_groups=plane)
    parts = call("merge_plane", merge_kernel, shape(len(depth[0]), 1, 6 * ncols), (), (parts,))
    parts = lax.all_to_all(parts, AXES, 0, 0, axis_index_groups=depth)
    rows, ok = call(
        "judge", judge_kernel, (shape(8, ncols), shape(1, 1, kind=jnp.int32)), (), (parts,), out_place=(VMEM, SMEM)
    )

    def combined(rows, p, q, *_):
        return call("combine", combine_kernel, shape(nrows, ncols), (), (rows, p, q)), rows[2]

    def normalised(rows, p, q, *args):
        return normalised_solve(*args)

    answer, miss = lax.cond(
        ok[0, 0] == 1, combined, normalised, rows, search_one, search_two, rhs, blocks, coupling, inverse,
        deflation, counts, panel, intersection_rows,
    )
    return (answer[None, None], miss)


def sum_groups(mesh):
    n_sub, n_blk = mesh.shape["sub"], mesh.shape["blk"]
    near = min(8, n_sub)
    size = near * n_blk
    count = n_sub // near
    plane = [[g * size + k for k in range(size)] for g in range(count)]
    depth = [[g * size + k for g in range(count)] for k in range(size)]
    return plane, depth


def solution(mesh):
    placed = (
        P("sub", "blk", None, None),
        P("sub", "blk", None, None, None),
        P("sub", "blk", None, None, None),
        P("sub", "blk", None, None, None),
        P("sub", "blk", None, None),
        P("sub", "blk"),
        P("sub", None, None),
        P("sub", "blk", None),
    )
    return jax.shard_map(
        functools.partial(body, mesh),
        mesh=mesh,
        in_specs=placed,
        out_specs=(P("sub", "blk", None, None), P()),
        check_vma=False,
    )
```

```python
import functools

import jax
import jax.numpy as jnp
from jax import lax
from jax.experimental import pallas as pl
from jax.experimental.pallas import tpu as pltpu
from jax.sharding import PartitionSpec as P

f32 = jnp.float32
bf16 = jnp.bfloat16
AXES = ("sub", "blk")
WIDE = 128
LEAST, MOST = 1e-12, 1e24
LIMIT = 24 * 1024 * 1024


def split(a):
    high = a.astype(bf16)
    return high, (a - high.astype(f32)).astype(bf16)


def dot(a, b, dims=((1,), (0,))):
    return lax.dot_general(a, b, (dims, ((), ())), preferred_element_type=f32)


def mul(a, b, dims=((1,), (0,))):
    return dot(a[0], b[0], dims) + (dot(a[0], b[1], dims) + dot(a[1], b[0], dims))


def pick(onehot, b):
    return dot(onehot, b[0]) + dot(onehot, b[1])


def gather_matrix(idx, nrows):
    count = idx.shape[1]
    column = jnp.broadcast_to(idx.astype(f32), (128, count)).T
    lane = lax.broadcasted_iota(jnp.int32, (count, 128), 1).astype(f32)
    parts = [
        jnp.where(column == lane + float(128 * k), 1.0, 0.0).astype(bf16)
        for k in range(nrows // 128)
    ]
    return jnp.concatenate(parts, axis=1)


def scatter_matrix(idx, nrows):
    row = lax.broadcasted_iota(jnp.int32, (nrows, idx.shape[1]), 0)
    return jnp.where(row == idx, 1.0, 0.0).astype(bf16)


def masked_deflation(defl, count):
    row = lax.broadcasted_iota(jnp.int32, defl.shape, 0)
    return jnp.where(row < count, defl, 0.0)


def edge_block(high, ref, width):
    start = pl.multiple_of(jnp.where(high, ref.shape[0] - width, 0), width)
    return ref[pl.ds(start, width)]


def padded(a, count):
    return jnp.concatenate([a, jnp.zeros((count - a.shape[0], a.shape[1]), a.dtype)], 0)


def tripled(high, low):
    return padded(jnp.concatenate([high, high, low], 0), WIDE).astype(bf16)


def gather_all(gather_ref, many, lines, a):
    high, low = split(a)
    top = dot(gather_ref[...], high)
    rest = dot(gather_ref[: many + lines], low)
    return top[:many] + rest[:many], top[many : many + lines] + (top[many + lines :] + rest[many:])


def prep_kernel(
    count_ref, odd_ref, slot_ref, r_hbm, idx_hbm, defl_hbm, inv_hbm,
    far_ref, near_ref, coef_ref, r_ref, inv_ref, gather_ref, scatter_ref, zrows_ref, lift_ref, off_ref,
    idx_ref, defl_ref, sems,
):
    many = idx_ref.shape[1]
    half = many // 2
    nrows, ncols = r_ref.shape
    kmax = defl_ref.shape[0]
    lines = zrows_ref.shape[0] // 2
    step = nrows // 4
    blocks, width = inv_ref.shape[0], inv_ref.shape[2]
    odd = odd_ref[0] == 1
    pieces = [(idx_hbm, idx_ref), (defl_hbm, defl_ref)]
    pieces += [(r_hbm.at[pl.ds(k * step, step)], r_ref.at[pl.ds(k * step, step)]) for k in range(4)]
    pieces += [(inv_hbm.at[k], inv_ref.at[k]) for k in (0, blocks - 1)]
    pieces += [(inv_hbm.at[pl.ds(1, blocks - 2)], inv_ref.at[pl.ds(1, blocks - 2)])]
    copies = [pltpu.make_async_copy(a, b, sems.at[k]) for k, (a, b) in enumerate(pieces)]
    for copy in copies:
        copy.start()
    copies[0].wait()
    low, high = idx_ref[:, :half], idx_ref[:, half:]
    idx = jnp.concatenate([jnp.where(odd, low, high), jnp.where(odd, high, low)], 1)
    gather = gather_matrix(idx, nrows)
    scatter = scatter_matrix(idx, nrows)
    gather_ref[:many] = gather
    scatter_ref[:, :many] = scatter
    off_ref[...] = 1.0 - dot(scatter, jnp.ones((many, off_ref.shape[1]), bf16))
    copies[1].wait()
    masked = masked_deflation(defl_ref[...], count_ref[0, 0])
    z_high = masked.astype(bf16).astype(f32)
    z_low = (masked - z_high).astype(bf16).astype(f32)
    z_pair = jnp.concatenate([padded(z_high, lines), padded(z_low, lines)], 0).astype(bf16)
    gather_ref[many:] = z_pair
    zrows_ref[...] = dot(z_pair, scatter).astype(bf16)
    lift = padded(jnp.concatenate([z_high, z_low, z_high], 0), WIDE).T.astype(bf16)
    scatter_ref[:, many:] = lift
    lift_ref[...] = dot(gather, lift).astype(bf16)
    for copy in copies[2:6]:
        copy.wait()
    rows, coef = gather_all(gather_ref, many, lines, r_ref[...])
    for k in range(coef_ref.shape[0]):
        coef_ref[k] = coef[:kmax]
    copies[6].wait()
    copies[7].wait()
    for k, (ref, high) in enumerate(((near_ref, odd_ref[0] == 0), (far_ref, odd))):
        ref[:half] = rows[k * half : (k + 1) * half]
        ref[half : 2 * half] = edge_block(high, r_ref, half)
        first, last = inv_ref[0, :half], inv_ref[blocks - 1, width - half :]
        ref[2 * half :, :half] = jnp.where(high, last[:, half:], first[:, :half])
        ref[2 * half :, half:] = jnp.where(high, last[:, :half], first[:, half:])
    copies[8].wait()


def local_kernel(
    odd_ref, slot_ref, r_ref, far_ref, near_ref, gfar_ref, gnear_ref, inv_far_ref, inv_near_ref,
    inv_ref, all_ref, panel_ref, lift_ref, gather_ref, own_ref, back_ref, coarse_ref, zfar_ref, znear_ref,
):
    odd = odd_ref[0] == 1
    half = znear_ref.shape[0]
    nrows, ncols = r_ref.shape
    kmax = all_ref.shape[1]
    width = inv_ref.shape[1]
    last = inv_ref.shape[0] - 1
    slot = pl.multiple_of(slot_ref[0] * kmax, 8)
    panel = split(panel_ref[pl.ds(slot, kmax), :])
    coefs = split(all_ref[...].reshape(all_ref.shape[0] * kmax, ncols))
    coarse = mul(panel, coefs)
    high = coarse.astype(bf16).astype(f32)
    coarse = tripled(high, coarse - high)
    coarse_ref[...] = coarse
    rows = dot(lift_ref[...], coarse)
    got_lo = jnp.where(odd, gnear_ref[:half], gfar_ref[:half])
    got_hi = jnp.where(odd, gfar_ref[:half], gnear_ref[:half])
    for n in range(last + 1):
        low = half if n == 0 else 0
        high = width - half if n == last else width
        if n == 0:
            part = jnp.concatenate([got_lo, r_ref[:half]], 0)
        elif n == last:
            part = jnp.concatenate([r_ref[nrows - half :], got_hi], 0)
        else:
            part = r_ref[n * width - half : (n + 1) * width - half]
        at = slice(n * width + low - half, n * width + high - half)
        y = mul(split(inv_ref[n, low:high]), split(part))
        own_ref[at] = y
        rows = rows + pick(gather_ref[: 2 * half, at], split(y))
    back = [
        mul(split(inverse[2 * half :]), split(jnp.concatenate([own[:half], got[half : 2 * half]], 0)))
        for own, got, inverse in ((near_ref, gnear_ref, inv_near_ref), (far_ref, gfar_ref, inv_far_ref))
    ]
    back = jnp.concatenate(back, 0)
    back_ref[...] = back
    rows = rows + back
    znear_ref[...] = rows[:half]
    zfar_ref[...] = rows[half:]


def block_products(own_ref, back_ref, coarse_ref, mats_ref, scatter_ref, z_ref, t_ref):
    many = back_ref.shape[0]
    high, low = split(back_ref[...])
    width = mats_ref.shape[1]
    both = jnp.concatenate([high, coarse_ref[...]], 0)
    for n in range(mats_ref.shape[0]):
        part = slice(n * width, (n + 1) * width)
        z = own_ref[part] + (dot(scatter_ref[part], both) + dot(scatter_ref[part, :many], low))
        z_ref[part] = z
        t_ref[part] = mul(split(mats_ref[n]), split(z))


def blocks_kernel(
    own_ref, back_ref, coarse_ref, mats_ref, scatter_ref, gather_ref, z_ref, t_ref, rows_ref, coef_ref
):
    block_products(own_ref, back_ref, coarse_ref, mats_ref, scatter_ref, z_ref, t_ref)
    rows_ref[...], coef = gather_all(gather_ref, rows_ref.shape[0], coef_ref.shape[0], t_ref[...])
    coef_ref[...] = coef


def shared_rows(odd_ref, couple_ref, gfar_ref, gnear_ref):
    near = mul(split(couple_ref[1 - odd_ref[0]]), split(gnear_ref[...]))
    far = mul(split(couple_ref[odd_ref[0]]), split(gfar_ref[...]))
    return jnp.concatenate([near, far], 0)


def image_kernel(
    odd_ref, t_ref, rows_ref, tcoef_ref, zrows_ref, couple_ref, gfar_ref, gnear_ref, scatter_ref,
    u_ref, far_ref, near_ref, coef_ref, urows_ref,
):
    add = shared_rows(odd_ref, couple_ref, gfar_ref, gnear_ref)
    many = add.shape[0]
    half = many // 2
    lines = tcoef_ref.shape[0]
    rows = rows_ref[...] + add
    urows_ref[...] = rows
    high, low = split(add)
    u_ref[...] = t_ref[...] + (dot(scatter_ref[:, :many], high) + dot(scatter_ref[:, :many], low))
    near_ref[:half] = rows[:half]
    far_ref[:half] = rows[half:]
    near_ref[half:] = edge_block(odd_ref[0] == 0, u_ref, half)
    far_ref[half:] = edge_block(odd_ref[0] == 1, u_ref, half)
    coef = dot(zrows_ref[...], high)
    coef = tcoef_ref[...] + (coef[:lines] + (coef[lines:] + dot(zrows_ref[:lines], low)))
    for k in range(coef_ref.shape[0]):
        coef_ref[k] = coef[: coef_ref.shape[1]]


highest = lax.Precision.HIGHEST


def with_halo(array, sides, width):
    for axis, dim in sides:
        peers, length = (lax.axis_size(axis), array.shape[dim])
        up = [(i, (i + 1) % peers) for i in range(peers - 1)]
        down = [(j, i) for i, j in up]
        last = lax.slice_in_dim(array, length - width, length, axis=dim)
        first = lax.slice_in_dim(array, 0, width, axis=dim)
        before = lax.ppermute(last, axis, up)
        after = lax.ppermute(first, axis, down)
        array = jnp.concatenate([before, array, after], axis=dim)
    return array


def apply_operator(field, block_mats, couple, low_idx, high_idx):
    half = low_idx.shape[0]
    sent = jnp.concatenate([field[low_idx], field[high_idx]], 0)
    padded = with_halo(sent, (("sub", 0),), half)
    from_low = padded[:half]
    from_high = padded[padded.shape[0] - half :]
    count_blocks, width = (block_mats.shape[0], block_mats.shape[1])
    local = jnp.einsum(
        "nij,njr->nir",
        block_mats,
        field.reshape(count_blocks, width, field.shape[1]),
        precision=highest,
    )
    local = local.reshape(field.shape)
    local = local.at[low_idx].add(jnp.dot(couple[0], from_low, precision=highest))
    return local.at[high_idx].add(jnp.dot(couple[1], from_high, precision=highest))


def apply_precond(resid, inv_mats, masked, panel_mat, low_idx, high_idx):
    half = low_idx.shape[0]
    nrows, ncols = resid.shape
    sent = jnp.concatenate([resid[low_idx], resid[high_idx]], 0)
    padded = with_halo(sent, (("sub", 0),), half)
    extended = jnp.concatenate([padded[:half], resid, padded[padded.shape[0] - half :]], 0)
    count_blocks, width = (inv_mats.shape[0], inv_mats.shape[1])
    solved = jnp.einsum(
        "nij,njr->nir", inv_mats, extended.reshape(count_blocks, width, ncols), precision=highest
    )
    solved = solved.reshape(nrows + 2 * half, ncols)
    own = solved[half : half + nrows]
    back_low = solved[:half]
    back_high = solved[half + nrows :]
    coef = jnp.dot(masked, resid, precision=highest)
    kmax = coef.shape[0]
    slot = lax.axis_index("blk")
    every = lax.all_gather(coef, "blk", axis=0, tiled=True)
    mine = lax.dynamic_slice_in_dim(panel_mat, slot * kmax, kmax, 0)
    correct = jnp.dot(mine, every, precision=highest)
    partial_value = own + jnp.einsum("kn,kr->nr", masked, correct, precision=highest)
    back = jnp.concatenate([back_low, back_high], 0)
    returned = with_halo(back, (("sub", 0),), half)
    field = partial_value.at[low_idx].add(returned[:half])
    field = field.at[high_idx].add(returned[returned.shape[0] - half :])
    return (field, None)


def normalised_solve(rhs, blocks, coupling, inverse, deflation, counts, panel, intersection_rows):
    source = rhs[0, 0]
    block_mats = blocks[0, 0]
    couple = coupling[0, 0]
    inv_mats = inverse[0, 0]
    panel_mat = panel[0]
    index_rows = intersection_rows[0, 0]
    half = index_rows.shape[0] // 2
    low_idx = index_rows[:half]
    high_idx = index_rows[half:]
    kmax = deflation.shape[2]
    keep = (jnp.arange(kmax, dtype=jnp.int32) < counts[0, 0]).astype(jnp.float32)
    masked = deflation[0, 0] * keep[:, None]

    def precond(vector):
        return apply_precond(vector, inv_mats, masked, panel_mat, low_idx, high_idx)

    def operator(vector):
        return apply_operator(vector, block_mats, couple, low_idx, high_idx)

    norm_sq = lax.psum(jnp.sum(source * source, 0), ("sub", "blk"))
    beta = jnp.sqrt(norm_sq)
    basis_one = source / beta
    search_one, rows_one = precond(basis_one)
    image = operator(search_one)
    proj_one, image_sq = lax.psum(
        (jnp.sum(image * basis_one, 0), jnp.sum(image * image, 0)), ("sub", "blk")
    )
    sub_one = jnp.sqrt(image_sq - proj_one * proj_one)
    basis_two = (image - proj_one * basis_one) / sub_one
    search_two, rows_two = precond(basis_two)
    image_two = operator(search_two)
    proj_two_a, proj_two_b, image_two_sq = lax.psum(
        (
            jnp.sum(image_two * basis_one, 0),
            jnp.sum(image_two * basis_two, 0),
            jnp.sum(image_two * image_two, 0),
        ),
        ("sub", "blk"),
    )
    sub_two = jnp.sqrt(image_two_sq - proj_two_a * proj_two_a - proj_two_b * proj_two_b)
    coeff_one, coeff_two, miss = least_squares(
        beta, proj_one, sub_one, proj_two_a, proj_two_b, sub_two
    )
    solution = coeff_one * search_one + coeff_two * search_two
    return (solution, miss[None])


def inverse_or_zero(a):
    return jnp.where(a > 0.0, 1.0 / jnp.where(a > 0.0, a, 1.0), 0.0)


def total(a):
    return jnp.sum(a, axis=0, keepdims=True)


PAIRS = ((0, 1), (0, 2), (1, 2))


def stacked(rows):
    return jnp.concatenate(rows + [jnp.zeros_like(rows[0])] * (8 - len(rows)), 0)


def last_blocks_kernel(
    own_ref, back_ref, coarse_ref, mats_ref, scatter_ref, gather_ref, off_ref,
    u0_ref, u1_ref, far0_ref, near0_ref, rows1_ref,
    z_ref, rows_ref, unit0_ref, unit1_ref, sums_ref, t_ref,
):
    many, ncols = rows_ref.shape
    half = many // 2
    nrows = z_ref.shape[0]
    lanes = off_ref.shape[1]
    block_products(own_ref, back_ref, coarse_ref, mats_ref, scatter_ref, z_ref, t_ref)
    rows_ref[...] = pick(gather_ref[:many], split(t_ref[...]))
    for at in range(0, nrows, 8):
        keep = off_ref[at : at + 8]
        for col in range(0, ncols, lanes):
            t_ref[at : at + 8, col : col + lanes] *= keep
    tops, factors = [], []
    for ref in (u0_ref, u1_ref, t_ref):
        top = jnp.max(jnp.abs(ref[...]).reshape(nrows // 8, 8, ncols), axis=0)
        top = jnp.max(top, axis=0, keepdims=True)
        tops.append(top)
        factors.append(inverse_or_zero(top))
    pairs = ((0, 0), (1, 1), (0, 1), (2, 2), (0, 2), (1, 2))
    sums = [jnp.zeros((8, ncols), f32)] * len(pairs)
    for at in range(0, nrows, 8):
        now = [ref[at : at + 8] * factor for ref, factor in zip((u0_ref, u1_ref, t_ref), factors)]
        sums = [total_ + now[i] * now[j] for total_, (i, j) in zip(sums, pairs)]
    sum_00, sum_11, sum_01, sum_22, sum_02, sum_12 = (total(a) for a in sums)
    size0, size1 = jnp.sqrt(sum_00), jnp.sqrt(sum_11)
    shrink0, shrink1 = inverse_or_zero(size0), inverse_or_zero(size1)
    unit0_ref[:half] = near0_ref[:half] * factors[0] * shrink0
    unit0_ref[half:] = far0_ref[:half] * factors[0] * shrink0
    unit1_ref[...] = rows1_ref[...] * factors[1] * shrink1
    sums_ref[...] = stacked(
        [
            tops[0] * size0, tops[1] * size1, tops[2], sum_01 * shrink0 * shrink1,
            sum_22, sum_02 * shrink0, sum_12 * shrink1,
        ]
    )


def gram_kernel(odd_ref, rows_ref, couple_ref, gfar_ref, gnear_ref, unit0_ref, unit1_ref, sums_ref, out_ref):
    rows = rows_ref[...] + shared_rows(odd_ref, couple_ref, gfar_ref, gnear_ref)
    len0, len1, top_off, cos_01, sum_22, sum_02, sum_12 = (sums_ref[k : k + 1] for k in range(7))
    top = jnp.maximum(top_off, jnp.max(jnp.abs(rows), axis=0, keepdims=True))
    scale = inverse_or_zero(top)
    rows = rows * scale
    ratio = top_off * scale
    size = jnp.sqrt(sum_22 * (ratio * ratio) + total(rows * rows))
    shrink = inverse_or_zero(size)
    cos_02 = (sum_02 * ratio + total(unit0_ref[...] * rows)) * shrink
    cos_12 = (sum_12 * ratio + total(unit1_ref[...] * rows)) * shrink
    send_packed([len0, len1, top * size, cos_01, cos_02, cos_12], out_ref)


def merge(parts):
    lengths, shares = [], []
    for own in parts[:3]:
        top = jnp.max(own, axis=0, keepdims=True)
        share = own * inverse_or_zero(top)
        size = jnp.sqrt(total(share * share))
        lengths.append(top * size)
        shares.append(share * inverse_or_zero(size))
    cosines = [
        total(parts[3 + k] * shares[i] * shares[j])
        for k, (i, j) in enumerate(PAIRS)
    ]
    return lengths, cosines


def unpacked(ref):
    ncols = ref.shape[2] // 6
    return [ref[:, 0, k * ncols : (k + 1) * ncols] for k in range(6)]


def send_packed(rows, ref):
    full = jnp.concatenate(rows, 1)
    for k in range(ref.shape[0]):
        ref[k] = full


def merge_kernel(parts_ref, out_ref):
    lengths, cosines = merge(unpacked(parts_ref))
    send_packed(lengths + cosines, out_ref)


def least_squares(beta, proj_one, sub_one, proj_two_a, proj_two_b, sub_two):
    diag_one = jnp.sqrt(proj_one * proj_one + sub_one * sub_one)
    cross = (proj_one * proj_two_a + sub_one * proj_two_b) / diag_one
    rest_a = proj_two_a - cross * proj_one / diag_one
    rest_b = proj_two_b - cross * sub_one / diag_one
    diag_two = jnp.sqrt(rest_a * rest_a + rest_b * rest_b + sub_two * sub_two)
    coeff_two = beta * rest_a / (diag_two * diag_two)
    coeff_one = (beta * proj_one / diag_one - cross * coeff_two) / diag_one
    miss_a = beta - proj_one * coeff_one - proj_two_a * coeff_two
    miss_b = sub_one * coeff_one + proj_two_b * coeff_two
    miss_c = sub_two * coeff_two
    miss = jnp.sqrt(miss_a * miss_a + miss_b * miss_b + miss_c * miss_c)
    return (coeff_one, coeff_two, miss)


def judge_kernel(parts_ref, rows_ref, ok_ref):
    (beta, len_one, len_two), (cos_01, cos_02, cos_12) = merge(unpacked(parts_ref))
    rel_one = len_one / beta
    proj_one = rel_one * cos_01
    sine_sq = 1.0 - cos_01 * cos_01
    sub_one = rel_one * jnp.sqrt(sine_sq)
    rel_two = len_two / beta / sub_one
    proj_two_a = rel_two * cos_02 - proj_one * (proj_one / sub_one)
    side = (cos_12 - cos_01 * cos_02) / jnp.sqrt(sine_sq)
    proj_two_b = rel_two * side - proj_one
    sub_two = rel_two * jnp.sqrt(1.0 - cos_02 * cos_02 - side * side)
    coeff_one, coeff_two, miss = least_squares(beta, proj_one, sub_one, proj_two_a, proj_two_b, sub_two)
    second = coeff_two / sub_one
    first = (coeff_one - second * proj_one) / beta
    rows_ref[...] = stacked([first, second / beta, miss])
    good = jnp.where(first * 0.0 + second * 0.0 + miss * 0.0 == 0.0, 1.0, 0.0)
    for a in (beta, len_one, len_two):
        good = jnp.where((a > LEAST) & (a < MOST), good, 0.0)
    ok_ref[0, 0] = jnp.where(jnp.min(good) > 0.0, 1, 0)


def combine_kernel(rows_ref, p_ref, q_ref, out_ref, miss_ref):
    miss_ref[...] = rows_ref[2:3]
    out_ref[...] = rows_ref[0:1] * p_ref[...] + rows_ref[1:2] * q_ref[...]


def shape(*dims, kind=f32):
    return jax.ShapeDtypeStruct(dims, kind)


VMEM = pl.BlockSpec(memory_space=pltpu.VMEM)
SMEM = pl.BlockSpec(memory_space=pltpu.SMEM)
HBM = pl.BlockSpec(memory_space=pltpu.HBM)


def call(name, kernel, out_shape, scalars, operands, place=VMEM, flops=0, scratch=(), out_place=None):
    size = sum(4 * a.size for a in operands)
    return pl.pallas_call(
        kernel,
        out_shape=out_shape,
        in_specs=[SMEM] * len(scalars) + [place] * len(operands),
        scratch_shapes=scratch,
        **({} if out_place is None else {"out_specs": out_place}),
        compiler_params=pltpu.CompilerParams(vmem_limit_bytes=LIMIT),
        cost_estimate=pl.CostEstimate(flops=flops, bytes_accessed=size, transcendentals=0),
        name=name,
    )(*scalars, *operands)


def body(mesh, rhs, blocks, coupling, inverse, deflation, counts, panel, intersection_rows):
    source, mats, couple, inv = rhs[0, 0], blocks[0, 0], coupling[0, 0], inverse[0, 0]
    defl, panel_mat = deflation[0, 0], panel[0]
    idx = intersection_rows[0]
    many = idx.shape[1]
    half = many // 2
    nrows, ncols = source.shape
    kmax = defl.shape[0]
    n_sub, n_blk = mesh.shape["sub"], mesh.shape["blk"]
    odd = jnp.bitwise_and(lax.axis_index("sub").astype(jnp.int32), 1)[None]
    slot = lax.axis_index("blk").astype(jnp.int32)[None]
    near_pairs = [(i, i ^ 1) for i in range(n_sub) if i ^ 1 < n_sub]
    far_pairs = [(i, ((i + 1) ^ 1) - 1) for i in range(1, n_sub) if ((i + 1) ^ 1) - 1 < n_sub]

    def halo(far, near):
        far = lax.ppermute(far, "sub", far_pairs)
        return far, lax.ppermute(near, "sub", near_pairs)

    def precond(vector, sent, got, coef):
        coefs = lax.all_to_all(coef, "blk", 0, 0)
        *parts, far, near = call(
            "local_solve", local_kernel,
            (
                shape(nrows, ncols), shape(many, ncols), shape(WIDE, ncols, kind=bf16), shape(half, ncols),
                shape(half, ncols),
            ),
            (odd, slot), (vector, *sent, *got, *inv_halves, inv, coefs, panel_mat, lift, gather),
            flops=10**9,
        )
        return parts, (far, near)

    lines = -(-kmax // 16) * 16
    *sent, coef, source, inv, gather, scatter, zrows, lift, off = call(
        "first_rows", prep_kernel,
        (
            shape(3 * half, ncols), shape(3 * half, ncols), shape(n_blk, kmax, ncols), shape(nrows, ncols),
            shape(*inv.shape), shape(many + 2 * lines, nrows, kind=bf16), shape(nrows, many + WIDE, kind=bf16),
            shape(2 * lines, many, kind=bf16), shape(many, WIDE, kind=bf16), shape(nrows, 128),
        ),
        (counts, odd, slot), [pltpu.with_memory_space_constraint(a, pltpu.HBM) for a in (source, idx, defl, inv)],
        place=HBM, flops=3 * 10**8, out_place=[VMEM] * 10,
        scratch=(pltpu.VMEM(idx.shape, jnp.int32), pltpu.VMEM(defl.shape, f32), pltpu.SemaphoreType.DMA((9,))),
    )
    got = inv_halves = halo(*sent)
    parts, halves = precond(source, sent, got, coef)
    z_got = halo(*halves)
    search_one, diag, diag_rows, diag_coef = call(
        "block_product", blocks_kernel,
        (shape(nrows, ncols), shape(nrows, ncols), shape(many, ncols), shape(lines, ncols)),
        (), (*parts, mats, scatter, gather), flops=10**9,
    )
    image, *sent_two, coef, image_rows = call(
        "image", image_kernel,
        (
            shape(nrows, ncols), shape(many, ncols), shape(many, ncols), shape(n_blk, kmax, ncols),
            shape(many, ncols),
        ),
        (odd,), (diag, diag_rows, diag_coef, zrows, couple, *z_got, scatter), flops=5 * 10**8,
    )
    got = halo(*sent_two)
    parts, halves = precond(image, sent_two, got, coef)
    z_got = halo(*halves)
    search_two, diag_rows, unit_one, unit_two, sums = call(
        "last_block_product", last_blocks_kernel,
        (shape(nrows, ncols), shape(many, ncols), shape(many, ncols), shape(many, ncols), shape(8, ncols)),
        (), (*parts, mats, scatter, gather, off, source, image, *sent, image_rows), flops=10**9,
        scratch=(pltpu.VMEM(source.shape, f32),),
    )
    plane, depth = sum_groups(mesh)
    parts = call(
        "lengths_cosines", gram_kernel, shape(len(plane[0]), 1, 6 * ncols),
        (odd,), (diag_rows, couple, *z_got, unit_one, unit_two, sums), flops=2 * 10**8,
    )
    parts = lax.all_to_all(parts, AXES, 0, 0, axis_index_groups=plane)
    parts = call("merge_plane", merge_kernel, shape(len(depth[0]), 1, 6 * ncols), (), (parts,))
    parts = lax.all_to_all(parts, AXES, 0, 0, axis_index_groups=depth)
    rows, ok = call(
        "judge", judge_kernel, (shape(8, ncols), shape(1, 1, kind=jnp.int32)), (), (parts,), out_place=(VMEM, SMEM)
    )

    def combined(rows, p, q, *_):
        return call("combine", combine_kernel, (shape(nrows, ncols), shape(1, ncols)), (), (rows, p, q))

    def normalised(rows, p, q, *args):
        return normalised_solve(*args)

    answer, miss = lax.cond(
        ok[0, 0] == 1, combined, normalised, rows, search_one, search_two, rhs, blocks, coupling, inverse,
        deflation, counts, panel, intersection_rows,
    )
    return (answer[None, None], miss[0])


def sum_groups(mesh):
    n_sub, n_blk = mesh.shape["sub"], mesh.shape["blk"]
    near = min(8, n_sub)
    size = near * n_blk
    count = n_sub // near
    plane = [[g * size + k for k in range(size)] for g in range(count)]
    depth = [[g * size + k for g in range(count)] for k in range(size)]
    return plane, depth


def solution(mesh):
    placed = (
        P("sub", "blk", None, None),
        P("sub", "blk", None, None, None),
        P("sub", "blk", None, None, None),
        P("sub", "blk", None, None, None),
        P("sub", "blk", None, None),
        P("sub", "blk"),
        P("sub", None, None),
        P("sub", "blk", None),
    )
    return jax.shard_map(
        functools.partial(body, mesh),
        mesh=mesh,
        in_specs=placed,
        out_specs=(P("sub", "blk", None, None), P()),
        check_vma=False,
    )
```

```python
import functools

import jax
import jax.numpy as jnp
from jax import lax
from jax.experimental import pallas as pl
from jax.experimental.pallas import tpu as pltpu
from jax.sharding import PartitionSpec as P

f32 = jnp.float32
bf16 = jnp.bfloat16
AXES = ("sub", "blk")
WIDE = 128
LEAST, MOST = 1e-12, 1e24
LIMIT = 24 * 1024 * 1024


def split(a):
    high = a.astype(bf16)
    return high, (a - high.astype(f32)).astype(bf16)


def dot(a, b, dims=((1,), (0,))):
    return lax.dot_general(a, b, (dims, ((), ())), preferred_element_type=f32)


def mul(a, b, dims=((1,), (0,))):
    return dot(a[0], b[0], dims) + (dot(a[0], b[1], dims) + dot(a[1], b[0], dims))


def pick(onehot, b):
    return dot(onehot, b[0]) + dot(onehot, b[1])


def gather_matrix(idx, nrows):
    count = idx.shape[1]
    column = jnp.broadcast_to(idx.astype(f32), (128, count)).T
    lane = lax.broadcasted_iota(jnp.int32, (count, 128), 1).astype(f32)
    parts = [
        jnp.where(column == lane + float(128 * k), 1.0, 0.0).astype(bf16)
        for k in range(nrows // 128)
    ]
    return jnp.concatenate(parts, axis=1)


def scatter_matrix(idx, nrows):
    row = lax.broadcasted_iota(jnp.int32, (nrows, idx.shape[1]), 0)
    return jnp.where(row == idx, 1.0, 0.0).astype(bf16)


def masked_deflation(defl, count):
    row = lax.broadcasted_iota(jnp.int32, defl.shape, 0)
    return jnp.where(row < count, defl, 0.0)


def edge_block(high, ref, width):
    start = pl.multiple_of(jnp.where(high, ref.shape[0] - width, 0), width)
    return ref[pl.ds(start, width)]


def padded(a, count):
    return jnp.concatenate([a, jnp.zeros((count - a.shape[0], a.shape[1]), a.dtype)], 0)


def tripled(high, low):
    return padded(jnp.concatenate([high, high, low], 0), WIDE).astype(bf16)


def gather_all(gather_ref, many, lines, a):
    high, low = split(a)
    top = dot(gather_ref[...], high)
    rest = dot(gather_ref[: many + lines], low)
    return top[:many] + rest[:many], top[many : many + lines] + (top[many + lines :] + rest[many:])


def prep_kernel(
    count_ref, odd_ref, slot_ref, r_hbm, idx_hbm, defl_hbm, inv_hbm,
    far_ref, near_ref, coef_ref, r_ref, inv_ref, gather_ref, scatter_ref, zrows_ref, lift_ref, off_ref,
    idx_ref, defl_ref, sems,
):
    many = idx_ref.shape[1]
    half = many // 2
    nrows, ncols = r_ref.shape
    kmax = defl_ref.shape[0]
    lines = zrows_ref.shape[0] // 2
    step = nrows // 4
    blocks, width = inv_ref.shape[0], inv_ref.shape[2]
    odd = odd_ref[0] == 1
    pieces = [(idx_hbm, idx_ref), (defl_hbm, defl_ref)]
    pieces += [(r_hbm.at[pl.ds(k * step, step)], r_ref.at[pl.ds(k * step, step)]) for k in range(4)]
    pieces += [(inv_hbm.at[k], inv_ref.at[k]) for k in (0, blocks - 1)]
    pieces += [(inv_hbm.at[pl.ds(1, blocks - 2)], inv_ref.at[pl.ds(1, blocks - 2)])]
    copies = [pltpu.make_async_copy(a, b, sems.at[k]) for k, (a, b) in enumerate(pieces)]
    for copy in copies:
        copy.start()
    copies[0].wait()
    low, high = idx_ref[:, :half], idx_ref[:, half:]
    idx = jnp.concatenate([jnp.where(odd, low, high), jnp.where(odd, high, low)], 1)
    gather = gather_matrix(idx, nrows)
    scatter = scatter_matrix(idx, nrows)
    gather_ref[:many] = gather
    scatter_ref[:, :many] = scatter
    off_ref[...] = 1.0 - dot(scatter, jnp.ones((many, off_ref.shape[1]), bf16))
    copies[1].wait()
    masked = masked_deflation(defl_ref[...], count_ref[0, 0])
    z_high = masked.astype(bf16).astype(f32)
    z_low = (masked - z_high).astype(bf16).astype(f32)
    z_pair = jnp.concatenate([padded(z_high, lines), padded(z_low, lines)], 0).astype(bf16)
    gather_ref[many:] = z_pair
    zrows_ref[...] = dot(z_pair, scatter).astype(bf16)
    lift = padded(jnp.concatenate([z_high, z_low, z_high], 0), WIDE).T.astype(bf16)
    scatter_ref[:, many:] = lift
    lift_ref[...] = dot(gather, lift).astype(bf16)
    for copy in copies[2:6]:
        copy.wait()
    rows, coef = gather_all(gather_ref, many, lines, r_ref[...])
    for k in range(coef_ref.shape[0]):
        coef_ref[k] = coef[:kmax]
    copies[6].wait()
    copies[7].wait()
    for k, (ref, high) in enumerate(((near_ref, odd_ref[0] == 0), (far_ref, odd))):
        ref[:half] = rows[k * half : (k + 1) * half]
        ref[half : 2 * half] = edge_block(high, r_ref, half)
        first, last = inv_ref[0, :half], inv_ref[blocks - 1, width - half :]
        ref[2 * half :, :half] = jnp.where(high, last[:, half:], first[:, :half])
        ref[2 * half :, half:] = jnp.where(high, last[:, :half], first[:, half:])
    copies[8].wait()


def local_kernel(
    odd_ref, slot_ref, r_ref, far_ref, near_ref, gfar_ref, gnear_ref, inv_far_ref, inv_near_ref,
    inv_ref, all_ref, panel_ref, lift_ref, gather_ref, own_ref, back_ref, coarse_ref, zfar_ref, znear_ref,
):
    odd = odd_ref[0] == 1
    half = znear_ref.shape[0]
    nrows, ncols = r_ref.shape
    kmax = all_ref.shape[1]
    width = inv_ref.shape[1]
    last = inv_ref.shape[0] - 1
    slot = pl.multiple_of(slot_ref[0] * kmax, 8)
    panel = split(panel_ref[pl.ds(slot, kmax), :])
    coefs = split(all_ref[...].reshape(all_ref.shape[0] * kmax, ncols))
    coarse = mul(panel, coefs)
    high = coarse.astype(bf16).astype(f32)
    coarse = tripled(high, coarse - high)
    coarse_ref[...] = coarse
    rows = dot(lift_ref[...], coarse)
    got_lo = jnp.where(odd, gnear_ref[:half], gfar_ref[:half])
    got_hi = jnp.where(odd, gfar_ref[:half], gnear_ref[:half])
    for n in range(last + 1):
        low = half if n == 0 else 0
        high = width - half if n == last else width
        if n == 0:
            part = jnp.concatenate([got_lo, r_ref[:half]], 0)
        elif n == last:
            part = jnp.concatenate([r_ref[nrows - half :], got_hi], 0)
        else:
            part = r_ref[n * width - half : (n + 1) * width - half]
        at = slice(n * width + low - half, n * width + high - half)
        y = mul(split(inv_ref[n, low:high]), split(part))
        own_ref[at] = y
        rows = rows + pick(gather_ref[: 2 * half, at], split(y))
    back = [
        mul(split(inverse[2 * half :]), split(jnp.concatenate([own[:half], got[half : 2 * half]], 0)))
        for own, got, inverse in ((near_ref, gnear_ref, inv_near_ref), (far_ref, gfar_ref, inv_far_ref))
    ]
    back = jnp.concatenate(back, 0)
    back_ref[...] = back
    rows = rows + back
    znear_ref[...] = rows[:half]
    zfar_ref[...] = rows[half:]


def block_products(own_ref, back_ref, coarse_ref, mats_ref, scatter_ref, z_ref, t_ref):
    many = back_ref.shape[0]
    high, low = split(back_ref[...])
    width = mats_ref.shape[1]
    both = jnp.concatenate([high, coarse_ref[...]], 0)
    for n in range(mats_ref.shape[0]):
        part = slice(n * width, (n + 1) * width)
        z = own_ref[part] + (dot(scatter_ref[part], both) + dot(scatter_ref[part, :many], low))
        z_ref[part] = z
        t_ref[part] = mul(split(mats_ref[n]), split(z))


def blocks_kernel(
    own_ref, back_ref, coarse_ref, mats_ref, scatter_ref, gather_ref, z_ref, t_ref, rows_ref, coef_ref
):
    block_products(own_ref, back_ref, coarse_ref, mats_ref, scatter_ref, z_ref, t_ref)
    rows_ref[...], coef = gather_all(gather_ref, rows_ref.shape[0], coef_ref.shape[0], t_ref[...])
    coef_ref[...] = coef


def shared_rows(odd_ref, couple_ref, gfar_ref, gnear_ref):
    near = mul(split(couple_ref[1 - odd_ref[0]]), split(gnear_ref[...]))
    far = mul(split(couple_ref[odd_ref[0]]), split(gfar_ref[...]))
    return jnp.concatenate([near, far], 0)


def image_kernel(
    odd_ref, t_ref, rows_ref, tcoef_ref, zrows_ref, couple_ref, gfar_ref, gnear_ref, scatter_ref,
    u_ref, far_ref, near_ref, coef_ref, urows_ref,
):
    add = shared_rows(odd_ref, couple_ref, gfar_ref, gnear_ref)
    many = add.shape[0]
    half = many // 2
    lines = tcoef_ref.shape[0]
    rows = rows_ref[...] + add
    urows_ref[...] = rows
    high, low = split(add)
    u_ref[...] = t_ref[...] + (dot(scatter_ref[:, :many], high) + dot(scatter_ref[:, :many], low))
    near_ref[:half] = rows[:half]
    far_ref[:half] = rows[half:]
    near_ref[half:] = edge_block(odd_ref[0] == 0, u_ref, half)
    far_ref[half:] = edge_block(odd_ref[0] == 1, u_ref, half)
    coef = dot(zrows_ref[...], high)
    coef = tcoef_ref[...] + (coef[:lines] + (coef[lines:] + dot(zrows_ref[:lines], low)))
    for k in range(coef_ref.shape[0]):
        coef_ref[k] = coef[: coef_ref.shape[1]]


highest = lax.Precision.HIGHEST


def with_halo(array, sides, width):
    for axis, dim in sides:
        peers, length = (lax.axis_size(axis), array.shape[dim])
        up = [(i, (i + 1) % peers) for i in range(peers - 1)]
        down = [(j, i) for i, j in up]
        last = lax.slice_in_dim(array, length - width, length, axis=dim)
        first = lax.slice_in_dim(array, 0, width, axis=dim)
        before = lax.ppermute(last, axis, up)
        after = lax.ppermute(first, axis, down)
        array = jnp.concatenate([before, array, after], axis=dim)
    return array


def apply_operator(field, block_mats, couple, low_idx, high_idx):
    half = low_idx.shape[0]
    sent = jnp.concatenate([field[low_idx], field[high_idx]], 0)
    padded = with_halo(sent, (("sub", 0),), half)
    from_low = padded[:half]
    from_high = padded[padded.shape[0] - half :]
    count_blocks, width = (block_mats.shape[0], block_mats.shape[1])
    local = jnp.einsum(
        "nij,njr->nir",
        block_mats,
        field.reshape(count_blocks, width, field.shape[1]),
        precision=highest,
    )
    local = local.reshape(field.shape)
    local = local.at[low_idx].add(jnp.dot(couple[0], from_low, precision=highest))
    return local.at[high_idx].add(jnp.dot(couple[1], from_high, precision=highest))


def apply_precond(resid, inv_mats, masked, panel_mat, low_idx, high_idx):
    half = low_idx.shape[0]
    nrows, ncols = resid.shape
    sent = jnp.concatenate([resid[low_idx], resid[high_idx]], 0)
    padded = with_halo(sent, (("sub", 0),), half)
    extended = jnp.concatenate([padded[:half], resid, padded[padded.shape[0] - half :]], 0)
    count_blocks, width = (inv_mats.shape[0], inv_mats.shape[1])
    solved = jnp.einsum(
        "nij,njr->nir", inv_mats, extended.reshape(count_blocks, width, ncols), precision=highest
    )
    solved = solved.reshape(nrows + 2 * half, ncols)
    own = solved[half : half + nrows]
    back_low = solved[:half]
    back_high = solved[half + nrows :]
    coef = jnp.dot(masked, resid, precision=highest)
    kmax = coef.shape[0]
    slot = lax.axis_index("blk")
    every = lax.all_gather(coef, "blk", axis=0, tiled=True)
    mine = lax.dynamic_slice_in_dim(panel_mat, slot * kmax, kmax, 0)
    correct = jnp.dot(mine, every, precision=highest)
    partial_value = own + jnp.einsum("kn,kr->nr", masked, correct, precision=highest)
    back = jnp.concatenate([back_low, back_high], 0)
    returned = with_halo(back, (("sub", 0),), half)
    field = partial_value.at[low_idx].add(returned[:half])
    field = field.at[high_idx].add(returned[returned.shape[0] - half :])
    return (field, None)


def normalised_solve(rhs, blocks, coupling, inverse, deflation, counts, panel, intersection_rows):
    source = rhs[0, 0]
    block_mats = blocks[0, 0]
    couple = coupling[0, 0]
    inv_mats = inverse[0, 0]
    panel_mat = panel[0]
    index_rows = intersection_rows[0, 0]
    half = index_rows.shape[0] // 2
    low_idx = index_rows[:half]
    high_idx = index_rows[half:]
    kmax = deflation.shape[2]
    keep = (jnp.arange(kmax, dtype=jnp.int32) < counts[0, 0]).astype(jnp.float32)
    masked = deflation[0, 0] * keep[:, None]

    def precond(vector):
        return apply_precond(vector, inv_mats, masked, panel_mat, low_idx, high_idx)

    def operator(vector):
        return apply_operator(vector, block_mats, couple, low_idx, high_idx)

    norm_sq = lax.psum(jnp.sum(source * source, 0), ("sub", "blk"))
    beta = jnp.sqrt(norm_sq)
    basis_one = source / beta
    search_one, rows_one = precond(basis_one)
    image = operator(search_one)
    proj_one, image_sq = lax.psum(
        (jnp.sum(image * basis_one, 0), jnp.sum(image * image, 0)), ("sub", "blk")
    )
    sub_one = jnp.sqrt(image_sq - proj_one * proj_one)
    basis_two = (image - proj_one * basis_one) / sub_one
    search_two, rows_two = precond(basis_two)
    image_two = operator(search_two)
    proj_two_a, proj_two_b, image_two_sq = lax.psum(
        (
            jnp.sum(image_two * basis_one, 0),
            jnp.sum(image_two * basis_two, 0),
            jnp.sum(image_two * image_two, 0),
        ),
        ("sub", "blk"),
    )
    sub_two = jnp.sqrt(image_two_sq - proj_two_a * proj_two_a - proj_two_b * proj_two_b)
    coeff_one, coeff_two, miss = least_squares(
        beta, proj_one, sub_one, proj_two_a, proj_two_b, sub_two
    )
    solution = coeff_one * search_one + coeff_two * search_two
    return (solution, miss[None])


def inverse_or_zero(a):
    return jnp.where(a > 0.0, 1.0 / jnp.where(a > 0.0, a, 1.0), 0.0)


def total(a):
    return jnp.sum(a, axis=0, keepdims=True)


PAIRS = ((0, 1), (0, 2), (1, 2))


def stacked(rows):
    return jnp.concatenate(rows + [jnp.zeros_like(rows[0])] * (8 - len(rows)), 0)


def last_blocks_kernel(
    own_ref, back_ref, coarse_ref, mats_ref, scatter_ref, gather_ref, off_ref,
    u0_ref, u1_ref, far0_ref, near0_ref, rows1_ref,
    z_ref, rows_ref, unit0_ref, unit1_ref, sums_ref, t_ref,
):
    many, ncols = rows_ref.shape
    half = many // 2
    nrows = z_ref.shape[0]
    lanes = off_ref.shape[1]
    block_products(own_ref, back_ref, coarse_ref, mats_ref, scatter_ref, z_ref, t_ref)
    rows_ref[...] = pick(gather_ref[:many], split(t_ref[...]))
    for at in range(0, nrows, 8):
        keep = off_ref[at : at + 8]
        for col in range(0, ncols, lanes):
            t_ref[at : at + 8, col : col + lanes] *= keep
    tops, factors = [], []
    for ref in (u0_ref, u1_ref, t_ref):
        top = jnp.max(jnp.abs(ref[...]).reshape(nrows // 8, 8, ncols), axis=0)
        top = jnp.max(top, axis=0, keepdims=True)
        tops.append(top)
        factors.append(inverse_or_zero(top))
    pairs = ((0, 0), (1, 1), (0, 1), (2, 2), (0, 2), (1, 2))
    sums = [jnp.zeros((8, ncols), f32)] * len(pairs)
    for at in range(0, nrows, 8):
        now = [ref[at : at + 8] * factor for ref, factor in zip((u0_ref, u1_ref, t_ref), factors)]
        sums = [total_ + now[i] * now[j] for total_, (i, j) in zip(sums, pairs)]
    sum_00, sum_11, sum_01, sum_22, sum_02, sum_12 = (total(a) for a in sums)
    size0, size1 = jnp.sqrt(sum_00), jnp.sqrt(sum_11)
    shrink0, shrink1 = inverse_or_zero(size0), inverse_or_zero(size1)
    unit0_ref[:half] = near0_ref[:half] * factors[0] * shrink0
    unit0_ref[half:] = far0_ref[:half] * factors[0] * shrink0
    unit1_ref[...] = rows1_ref[...] * factors[1] * shrink1
    sums_ref[...] = stacked(
        [
            tops[0] * size0, tops[1] * size1, tops[2], sum_01 * shrink0 * shrink1,
            sum_22, sum_02 * shrink0, sum_12 * shrink1,
        ]
    )


def gram_kernel(odd_ref, rows_ref, couple_ref, gfar_ref, gnear_ref, unit0_ref, unit1_ref, sums_ref, out_ref):
    rows = rows_ref[...] + shared_rows(odd_ref, couple_ref, gfar_ref, gnear_ref)
    len0, len1, top_off, cos_01, sum_22, sum_02, sum_12 = (sums_ref[k : k + 1] for k in range(7))
    top = jnp.maximum(top_off, jnp.max(jnp.abs(rows), axis=0, keepdims=True))
    scale = inverse_or_zero(top)
    rows = rows * scale
    ratio = top_off * scale
    size = jnp.sqrt(sum_22 * (ratio * ratio) + total(rows * rows))
    shrink = inverse_or_zero(size)
    cos_02 = (sum_02 * ratio + total(unit0_ref[...] * rows)) * shrink
    cos_12 = (sum_12 * ratio + total(unit1_ref[...] * rows)) * shrink
    send_packed([len0, len1, top * size, cos_01, cos_02, cos_12], out_ref)


def merge(parts):
    lengths, shares = [], []
    for own in parts[:3]:
        top = jnp.max(own, axis=0, keepdims=True)
        share = own * inverse_or_zero(top)
        size = jnp.sqrt(total(share * share))
        lengths.append(top * size)
        shares.append(share * inverse_or_zero(size))
    cosines = [
        total(parts[3 + k] * shares[i] * shares[j])
        for k, (i, j) in enumerate(PAIRS)
    ]
    return lengths, cosines


def unpacked(ref):
    ncols = ref.shape[2] // 6
    return [ref[:, 0, k * ncols : (k + 1) * ncols] for k in range(6)]


def send_packed(rows, ref):
    full = jnp.concatenate(rows, 1)
    for k in range(ref.shape[0]):
        ref[k] = full


def merge_kernel(parts_ref, out_ref):
    lengths, cosines = merge(unpacked(parts_ref))
    send_packed(lengths + cosines, out_ref)


def least_squares(beta, proj_one, sub_one, proj_two_a, proj_two_b, sub_two):
    diag_one = jnp.sqrt(proj_one * proj_one + sub_one * sub_one)
    cross = (proj_one * proj_two_a + sub_one * proj_two_b) / diag_one
    rest_a = proj_two_a - cross * proj_one / diag_one
    rest_b = proj_two_b - cross * sub_one / diag_one
    diag_two = jnp.sqrt(rest_a * rest_a + rest_b * rest_b + sub_two * sub_two)
    coeff_two = beta * rest_a / (diag_two * diag_two)
    coeff_one = (beta * proj_one / diag_one - cross * coeff_two) / diag_one
    miss_a = beta - proj_one * coeff_one - proj_two_a * coeff_two
    miss_b = sub_one * coeff_one + proj_two_b * coeff_two
    miss_c = sub_two * coeff_two
    miss = jnp.sqrt(miss_a * miss_a + miss_b * miss_b + miss_c * miss_c)
    return (coeff_one, coeff_two, miss)


def judge_kernel(parts_ref, p_ref, q_ref, out_ref, miss_ref, ok_ref):
    (beta, len_one, len_two), (cos_01, cos_02, cos_12) = merge(unpacked(parts_ref))
    rel_one = len_one / beta
    proj_one = rel_one * cos_01
    sine_sq = 1.0 - cos_01 * cos_01
    sub_one = rel_one * jnp.sqrt(sine_sq)
    rel_two = len_two / beta / sub_one
    proj_two_a = rel_two * cos_02 - proj_one * (proj_one / sub_one)
    side = (cos_12 - cos_01 * cos_02) / jnp.sqrt(sine_sq)
    proj_two_b = rel_two * side - proj_one
    sub_two = rel_two * jnp.sqrt(1.0 - cos_02 * cos_02 - side * side)
    coeff_one, coeff_two, miss = least_squares(beta, proj_one, sub_one, proj_two_a, proj_two_b, sub_two)
    second = coeff_two / sub_one
    first = (coeff_one - second * proj_one) / beta
    miss_ref[...] = miss
    out_ref[...] = first * p_ref[...] + (second / beta) * q_ref[...]
    good = jnp.where(first * 0.0 + second * 0.0 + miss * 0.0 == 0.0, 1.0, 0.0)
    for a in (beta, len_one, len_two):
        good = jnp.where((a > LEAST) & (a < MOST), good, 0.0)
    ok_ref[0, 0] = jnp.where(jnp.min(good) > 0.0, 1, 0)


def shape(*dims, kind=f32):
    return jax.ShapeDtypeStruct(dims, kind)


VMEM = pl.BlockSpec(memory_space=pltpu.VMEM)
SMEM = pl.BlockSpec(memory_space=pltpu.SMEM)
HBM = pl.BlockSpec(memory_space=pltpu.HBM)


def call(name, kernel, out_shape, scalars, operands, place=VMEM, flops=0, scratch=(), out_place=None):
    size = sum(4 * a.size for a in operands)
    return pl.pallas_call(
        kernel,
        out_shape=out_shape,
        in_specs=[SMEM] * len(scalars) + [place] * len(operands),
        scratch_shapes=scratch,
        **({} if out_place is None else {"out_specs": out_place}),
        compiler_params=pltpu.CompilerParams(vmem_limit_bytes=LIMIT),
        cost_estimate=pl.CostEstimate(flops=flops, bytes_accessed=size, transcendentals=0),
        name=name,
    )(*scalars, *operands)


def body(mesh, rhs, blocks, coupling, inverse, deflation, counts, panel, intersection_rows):
    source, mats, couple, inv = rhs[0, 0], blocks[0, 0], coupling[0, 0], inverse[0, 0]
    defl, panel_mat = deflation[0, 0], panel[0]
    idx = intersection_rows[0]
    many = idx.shape[1]
    half = many // 2
    nrows, ncols = source.shape
    kmax = defl.shape[0]
    n_sub, n_blk = mesh.shape["sub"], mesh.shape["blk"]
    odd = jnp.bitwise_and(lax.axis_index("sub").astype(jnp.int32), 1)[None]
    slot = lax.axis_index("blk").astype(jnp.int32)[None]
    near_pairs = [(i, i ^ 1) for i in range(n_sub) if i ^ 1 < n_sub]
    far_pairs = [(i, ((i + 1) ^ 1) - 1) for i in range(1, n_sub) if ((i + 1) ^ 1) - 1 < n_sub]

    def halo(far, near):
        far = lax.ppermute(far, "sub", far_pairs)
        return far, lax.ppermute(near, "sub", near_pairs)

    def precond(vector, sent, got, coef):
        coefs = lax.all_to_all(coef, "blk", 0, 0)
        *parts, far, near = call(
            "local_solve", local_kernel,
            (
                shape(nrows, ncols), shape(many, ncols), shape(WIDE, ncols, kind=bf16), shape(half, ncols),
                shape(half, ncols),
            ),
            (odd, slot), (vector, *sent, *got, *inv_halves, inv, coefs, panel_mat, lift, gather),
            flops=10**9,
        )
        return parts, (far, near)

    lines = -(-kmax // 16) * 16
    *sent, coef, source, inv, gather, scatter, zrows, lift, off = call(
        "first_rows", prep_kernel,
        (
            shape(3 * half, ncols), shape(3 * half, ncols), shape(n_blk, kmax, ncols), shape(nrows, ncols),
            shape(*inv.shape), shape(many + 2 * lines, nrows, kind=bf16), shape(nrows, many + WIDE, kind=bf16),
            shape(2 * lines, many, kind=bf16), shape(many, WIDE, kind=bf16), shape(nrows, 128),
        ),
        (counts, odd, slot), [pltpu.with_memory_space_constraint(a, pltpu.HBM) for a in (source, idx, defl, inv)],
        place=HBM, flops=3 * 10**8, out_place=[VMEM] * 10,
        scratch=(pltpu.VMEM(idx.shape, jnp.int32), pltpu.VMEM(defl.shape, f32), pltpu.SemaphoreType.DMA((9,))),
    )
    got = inv_halves = halo(*sent)
    parts, halves = precond(source, sent, got, coef)
    z_got = halo(*halves)
    search_one, diag, diag_rows, diag_coef = call(
        "block_product", blocks_kernel,
        (shape(nrows, ncols), shape(nrows, ncols), shape(many, ncols), shape(lines, ncols)),
        (), (*parts, mats, scatter, gather), flops=10**9,
    )
    image, *sent_two, coef, image_rows = call(
        "image", image_kernel,
        (
            shape(nrows, ncols), shape(many, ncols), shape(many, ncols), shape(n_blk, kmax, ncols),
            shape(many, ncols),
        ),
        (odd,), (diag, diag_rows, diag_coef, zrows, couple, *z_got, scatter), flops=5 * 10**8,
    )
    got = halo(*sent_two)
    parts, halves = precond(image, sent_two, got, coef)
    z_got = halo(*halves)
    search_two, diag_rows, unit_one, unit_two, sums = call(
        "last_block_product", last_blocks_kernel,
        (shape(nrows, ncols), shape(many, ncols), shape(many, ncols), shape(many, ncols), shape(8, ncols)),
        (), (*parts, mats, scatter, gather, off, source, image, *sent, image_rows), flops=10**9,
        scratch=(pltpu.VMEM(source.shape, f32),),
    )
    plane, depth = sum_groups(mesh)
    parts = call(
        "lengths_cosines", gram_kernel, shape(len(plane[0]), 1, 6 * ncols),
        (odd,), (diag_rows, couple, *z_got, unit_one, unit_two, sums), flops=2 * 10**8,
    )
    parts = lax.all_to_all(parts, AXES, 0, 0, axis_index_groups=plane)
    parts = call("merge_plane", merge_kernel, shape(len(depth[0]), 1, 6 * ncols), (), (parts,))
    parts = lax.all_to_all(parts, AXES, 0, 0, axis_index_groups=depth)
    answer, miss, ok = call(
        "judge", judge_kernel, (shape(nrows, ncols), shape(1, ncols), shape(1, 1, kind=jnp.int32)), (),
        (parts, search_one, search_two), out_place=(VMEM, VMEM, SMEM),
    )

    def kept(answer, miss, *_):
        return answer, miss

    def normalised(answer, miss, *args):
        return normalised_solve(*args)

    answer, miss = lax.cond(
        ok[0, 0] == 1, kept, normalised, answer, miss, rhs, blocks, coupling, inverse, deflation, counts, panel,
        intersection_rows,
    )
    return (answer[None, None], miss[0])


def sum_groups(mesh):
    n_sub, n_blk = mesh.shape["sub"], mesh.shape["blk"]
    near = min(8, n_sub)
    size = near * n_blk
    count = n_sub // near
    plane = [[g * size + k for k in range(size)] for g in range(count)]
    depth = [[g * size + k for g in range(count)] for k in range(size)]
    return plane, depth


def solution(mesh):
    placed = (
        P("sub", "blk", None, None),
        P("sub", "blk", None, None, None),
        P("sub", "blk", None, None, None),
        P("sub", "blk", None, None, None),
        P("sub", "blk", None, None),
        P("sub", "blk"),
        P("sub", None, None),
        P("sub", "blk", None),
    )
    return jax.shard_map(
        functools.partial(body, mesh),
        mesh=mesh,
        in_specs=placed,
        out_specs=(P("sub", "blk", None, None), P()),
        check_vma=False,
    )
```
